512 devices in a mesh: lat: 8 (over y_lo, x), lon: 64 (over z, y_hi, core).
Axes of the slice: x: 4, y: 4 (y_hi: 2, y_lo: 2; y = y_hi * 2 + y_lo), z: 16, core: 2. Of those that a mesh axis runs over, the one named last changes fastest.
Arguments:
- field_state: bfloat16 [4, 64, 163840], P(None, 'lat', 'lon'), may hold values from -6 to 6
- reservoir_state: bfloat16 [16, 1024, 4, 1024], P('lat', 'lon'), may hold values from -0.8984375 to 0.8984375
- coupling_blocks: bfloat16 [16, 2048, 128], P('lat'), may hold values from -0.375 to 0.375
- coupling_index: int32 [16, 8, 2], P('lat'), may hold values from 0 to 7, as said below
- input_blocks: bfloat16 [16, 1024, 128], P('lat'), may hold values from -0.5 to 0.5
- input_index: int32 [16, 8], P('lat'), may hold values from 0 to 19
- zonal_band_output_matrices: bfloat16 [8, 640, 1024], P('lat'), may hold values from -0.1875 to 0.1875
- region_band: int32 [16], P('lat'), may hold values from 0 to 1
Outputs:
- field_out: bfloat16 [4, 64, 163840], P(None, 'lat', 'lon')
- states_out: bfloat16 [16, 1024, 4, 1024], P('lat', 'lon')
The draws below stay inside these ranges and needn't reach their ends.
Inputs may be any that keep to these rules, and one draw needn't show every extreme that they name: `coupling_index`: the 2 block columns of one block-row differ. `region_band`: a band of the region row's own latitude group of 2 region rows.
All inputs are finite; a program needn't handle non-finite values.
Results may differ from the reference program's by a relative error of at most 0.0095.
Values may be sent and summed in bfloat16 or wider, within the bound.
A program may use at most 64 MiB of HBM per device.

```python
import jax
import jax.numpy as jnp
from jax import lax

UNITS = 1024
VARS = 40
BLK = 128
SLOTS = 2
BANDS_DEV = 2
MEMBERS = 4
STEPS = 3
REG_Y = 2
BANDS = 16
GROUPS = 8
OUTS = 640
LAT_REG = 16
LON_REG = 1024
LAT_CELLS = 64
LON_CELLS = 4096


def draw_coupling_index(key, part):
    key = jax.random.fold_in(key, 11)
    first_key, second_key = jax.random.split(key)
    block_rows = UNITS // BLK
    first = jax.random.randint(first_key, (BANDS, block_rows), 0, block_rows)
    offset = jax.random.randint(second_key, (BANDS, block_rows), 1, block_rows)
    second = (first + offset) % block_rows
    return jnp.stack([first, second], axis=-1).astype(jnp.int32)


def plant(values, rng, low, top_value):
    index_at = [jax.random.randint(jax.random.fold_in(rng, axis), (), 0, length) for axis, length in enumerate(values.shape)]
    longest = values.shape.index(max(values.shape))
    next_to = index_at[:longest] + [(index_at[longest] + 1) % values.shape[longest]] + index_at[longest + 1:]
    return values.at[tuple(index_at)].set(low).at[tuple(next_to)].set(top_value)


def steps_of(stream_key, dims, shards, least, top_value):
    factor_of, own = 1.0, jax.random.fold_in(stream_key, 6)
    for axis_at, blocks in shards:
        draws = jnp.exp(jax.random.uniform(jax.random.fold_in(own, axis_at), (blocks,), jnp.float32, least / len(shards), top_value / len(shards)))
        factor_of = factor_of * jnp.repeat(draws, dims[axis_at] // blocks).reshape([-1 if axis == axis_at else 1 for axis in range(len(dims))])
    return factor_of


def noise(rng, extent, spread, most, cuts=(), dtype=jnp.bfloat16):
    entries = jax.random.normal(rng, extent, jnp.float32) * spread
    if len(cuts) > 0:
        entries = steps_of(rng, extent, cuts, -0.22, 0.18) * entries
    return jnp.clip(entries, min=-most, max=most).astype(dtype)


def setup_inputs(seed: int = 0) -> dict:
    keys = jax.random.split(jax.random.key(seed), 9)
    field_state = noise(keys[0], (MEMBERS, LAT_CELLS, LON_CELLS * VARS), 1.0, 6.0, ((1, 8), (2, 64)))
    reservoir_state = jnp.clip(jax.random.uniform(keys[1], (LAT_REG, LON_REG, MEMBERS, UNITS), jnp.float32, -0.8984375, 0.8984375) * steps_of(keys[1], (LAT_REG, LON_REG, MEMBERS, UNITS), ((0, 8), (1, 64)), -0.4, 0.0), -0.8984375, 0.8984375).astype(jnp.bfloat16)
    coupling_blocks = noise(keys[2], (BANDS, UNITS * SLOTS, BLK), (SLOTS * BLK) ** -0.5, 0.375, ((0, 8),))
    coupling_index = draw_coupling_index(jax.random.fold_in(keys[8], 71), 0)
    input_blocks = noise(keys[4], (BANDS, UNITS, BLK), BLK ** -0.5, 0.5, ((0, 8),))
    input_index = plant(jax.random.randint(keys[5], (BANDS, UNITS // BLK), 0, 64 * VARS // BLK), jax.random.fold_in(keys[5], 1), 0, (64 * VARS // BLK) - 1).astype(jnp.int32)
    zonal_band_output_matrices = noise(keys[6], (GROUPS, OUTS, UNITS), UNITS ** -0.5, 0.1875, ((0, 8),))
    region_band = plant(jax.random.randint(keys[7], (LAT_REG,), 0, BANDS_DEV), jax.random.fold_in(keys[7], 1), 0, BANDS_DEV - 1).astype(jnp.int32)
    return dict(field_state=field_state, reservoir_state=reservoir_state, coupling_blocks=coupling_blocks, coupling_index=coupling_index, input_blocks=input_blocks, input_index=input_index, zonal_band_output_matrices=zonal_band_output_matrices, region_band=region_band)


def region_inputs(band_slab, region_count, vertical_quantity_total):
    perturbation_copies = band_slab.shape[0]
    pieces = band_slab.reshape(perturbation_copies, 8, region_count + 1, 4 * vertical_quantity_total)
    windows = jnp.concatenate([pieces[:, :, :-1], pieces[:, :, 1:]], axis=3)
    return windows.transpose(2, 0, 1, 3).reshape(region_count * perturbation_copies, 64 * vertical_quantity_total)


def reservoir_update(state_rows, input_rows, coupling, coupling_idx, driving, driving_idx):
    row_count = state_rows.shape[0]
    block_rows = coupling_idx.shape[0]
    slot_count = coupling_idx.shape[1]
    block_size = coupling.shape[-1]
    picked = jnp.take(state_rows.reshape(row_count, block_rows, block_size), coupling_idx, axis=1)
    blocks = coupling.reshape(block_rows, slot_count, block_size, block_size)
    recurrent = jnp.einsum("nbki,bkoi->nbo", picked.astype(jnp.float32), blocks.astype(jnp.float32))
    chosen = jnp.take(input_rows.reshape(row_count, -1, block_size), driving_idx, axis=1)
    drive_blocks = driving.reshape(block_rows, block_size, block_size)
    drive_term = jnp.einsum("nbi,boi->nbo", chosen.astype(jnp.float32), drive_blocks.astype(jnp.float32))
    refreshed_activation = jnp.tanh(recurrent + drive_term)
    return refreshed_activation.reshape(row_count, block_rows * block_size).astype(jnp.bfloat16)


def reference(field_state, reservoir_state, coupling_blocks, coupling_index, input_blocks, input_index, zonal_band_output_matrices, region_band):
    vertical_quantity_total = VARS
    perturbation_copies, lat_cells, flat_cols = field_state.shape
    meridional_sector_total = flat_cols // (4 * vertical_quantity_total)
    latitude_region_count = lat_cells // 4
    current = field_state
    states_now = reservoir_state
    for step_index in range(STEPS):
        padded = jnp.pad(current, ((0, 0), (2, 2), (0, 0)))
        padded = jnp.concatenate([padded[:, :, -2 * vertical_quantity_total:], padded, padded[:, :, :2 * vertical_quantity_total]], axis=2)
        gridpoint_line_entries = []
        state_rows = []
        for region_row in range(latitude_region_count):
            zonal_band_number = region_row // REG_Y
            band_index = zonal_band_number * BANDS_DEV + region_band[region_row]
            coupling = lax.dynamic_index_in_dim(coupling_blocks, band_index, 0, keepdims=False)
            coupling_idx = lax.dynamic_index_in_dim(coupling_index, band_index, 0, keepdims=False)
            driving = lax.dynamic_index_in_dim(input_blocks, band_index, 0, keepdims=False)
            driving_idx = lax.dynamic_index_in_dim(input_index, band_index, 0, keepdims=False)
            previous = states_now[region_row].reshape(meridional_sector_total * perturbation_copies, UNITS)
            inputs_now = region_inputs(padded[:, 4 * region_row:4 * region_row + 8], meridional_sector_total, vertical_quantity_total)
            refreshed_activation = reservoir_update(previous, inputs_now, coupling, coupling_idx, driving, driving_idx)
            prediction_sequence = jnp.dot(refreshed_activation, zonal_band_output_matrices[zonal_band_number].T, preferred_element_type=jnp.float32).astype(jnp.bfloat16)
            state_rows.append(refreshed_activation.reshape(meridional_sector_total, perturbation_copies, UNITS))
            gridpoint_line_entries.append(prediction_sequence.reshape(meridional_sector_total, perturbation_copies, 4, 4 * vertical_quantity_total).transpose(1, 2, 0, 3).reshape(perturbation_copies, 4, meridional_sector_total * 4 * vertical_quantity_total))
        current = jnp.concatenate(gridpoint_line_entries, axis=1)
        states_now = jnp.stack(state_rows, axis=0)
    return current, states_now
```

```python
import functools

import jax
import jax.numpy as jnp
from jax import lax
from jax.experimental import pallas as pl
from jax.experimental.pallas import tpu as pltpu
from jax.sharding import PartitionSpec as P

MESH = pl.DeviceIdType.MESH
STEPS = 3
F32 = jnp.float32
BF16 = jnp.bfloat16

DIRS = ((-1, 0), (1, 0), (0, -1), (0, 1), (-1, -1), (-1, 1), (1, -1), (1, 1))


def dot_nt(x, w):
    return lax.dot_general(x, w, (((1,), (1,)), ((), ())), preferred_element_type=F32)


def lanes(rows):
    return lax.broadcasted_iota(jnp.int32, (rows, 128), 1)


def roll(x, by):
    return pltpu.roll(x, by, 1)


def minus_parts(r0, r1, r2):
    lane = lanes(r0.shape[0])
    b0 = jnp.where(lane < 48, roll(r0, 48), roll(r1, 48))
    r2r = roll(r2, 80)
    b2 = jnp.where(lane < 80, roll(r1, 80), r2r)
    return b0, b2, r2r


def plus_parts(r0, r1):
    r0r = roll(r0, 112)
    return r0r, r0r, roll(r1, 16)


def windows(r0, r1, r2, n):
    rows = 8 * n
    lane = lanes(rows)
    m = slice(0, rows)
    c = slice(8, rows + 8)
    p = slice(16, rows + 16)
    m0, m2, m3 = minus_parts(r0[m], r1[m], r2[m])
    p1, p2, p4 = plus_parts(r0[p], r1[p])
    c0 = roll(r0[c], 80)
    c1 = roll(r1[c], 80)
    d1 = roll(r1[c], 112)
    d2 = roll(r2[c], 112)
    b0 = jnp.where(lane < 80, m0, c0)
    b1 = jnp.where(lane < 80, c0, jnp.where(lane < 112, c1, p1))
    b2 = jnp.where(lane < 64, p2, m2)
    b3 = jnp.where(lane < 16, m3, jnp.where(lane < 112, d1, d2))
    b4 = jnp.where(lane < 48, d2, p4)
    return b0, b1, b2, b3, b4


def kernel(
    cidx, qidx, rband,
    field_hbm, state_hbm, coup_hbm, drive_hbm, read_hbm,
    field_out, state_out,
    field_in, state_in, coup, drive, read,
    states, pre, win, raw, halo, edge, edge_in, ta, tb,
    local_sem, send_sem, recv_sem,
):
    lat, lon = lax.axis_index("lat"), lax.axis_index("lon")
    nlat, nlon = lax.axis_size("lat"), lax.axis_size("lon")
    west, east = lax.rem(lon + nlon - 1, nlon), lax.rem(lon + 1, nlon)
    has_south = lat > 0
    has_north = lat < nlat - 1

    def target(d):
        dl, do = DIRS[d]
        return (lat + dl, west if do < 0 else (east if do > 0 else lon))

    def by_side(fn):
        for d in (0, 4, 5, 1, 6, 7, 2, 3):
            dl = DIRS[d][0]
            if dl == 0:
                fn(d)
            else:
                pl.when(has_south if dl < 0 else has_north)(functools.partial(fn, d))

    barrier = pltpu.get_barrier_semaphore()
    by_side(lambda d: pl.semaphore_signal(barrier, inc=1, device_id=target(d), device_id_type=MESH))

    loads = [
        pltpu.make_async_copy(src, dst, local_sem.at[n])
        for n, (src, dst) in enumerate(
            ((field_hbm, field_in), (state_hbm, state_in), (coup_hbm, coup), (drive_hbm, drive), (read_hbm, read))
        )
    ]
    for load in loads:
        load.start()

    @pl.when(lat == 0)
    def _():
        halo[:, 0] = jnp.zeros(halo.shape[:1] + halo.shape[2:], BF16)
        edge_in[:, 6:8] = jnp.zeros((STEPS, 2) + edge_in.shape[2:], BF16)

    @pl.when(lat == nlat - 1)
    def _():
        halo[:, 1] = jnp.zeros(halo.shape[:1] + halo.shape[2:], BF16)
        edge_in[:, 4:6] = jnp.zeros((STEPS, 2) + edge_in.shape[2:], BF16)

    def message(step, d):
        if d == 0:
            src, dst = raw.at[step, 0], halo.at[step, 1]
        elif d == 1:
            src, dst = raw.at[step, 3], halo.at[step, 0]
        else:
            src, dst = edge.at[step, 0 if DIRS[d][1] < 0 else 1], edge_in.at[step, d]
        return pltpu.make_async_remote_copy(
            src_ref=src, dst_ref=dst, send_sem=send_sem.at[step, d], recv_sem=recv_sem.at[step, d],
            device_id=target(d), device_id_type=MESH,
        )

    def wait_recv(step, d):
        dl = DIRS[d][0]
        if dl == 0:
            message(step, d).wait_recv()
        else:
            @pl.when(has_north if dl < 0 else has_south)
            def _():
                message(step, d).wait_recv()

    def put_raw(step, pair, r):
        for k in range(3):
            raw[step, pair, k] = r[k].astype(BF16)

    def put_edges(step, rs):
        for k in range(3):
            first = jnp.concatenate([rs[p][k][0:4] for p in range(4)], axis=0)
            last = jnp.concatenate([rs[p][k][60:64] for p in range(4)], axis=0)
            edge[step, 0, k] = first.astype(BF16)
            edge[step, 1, k] = last.astype(BF16)

    def send(step):
        by_side(lambda d: message(step, d).start())

    loads[0].wait()
    lane8 = lanes(8)
    for m in range(4):
        f = [field_in[m, :, 128 * k:128 * (k + 1)].astype(F32) for k in range(20)]
        for j in range(16):
            q, off = (160 * j) // 128, (160 * j) % 128
            row = (j % 8) * 8 + (j // 8) * 4 + m
            if off == 0:
                w0, w1 = f[q], f[q + 1]
            else:
                w1 = roll(f[q + 1], 128 - off)
                w0 = jnp.where(lane8 < 128 - off, roll(f[q], 128 - off), w1)
            ta[pl.ds(row, 8, stride=64), :] = w0
            tb[pl.ds(row, 8, stride=64), :] = w1
    lane64 = lanes(64)
    rs = []
    for p in range(4):
        a0, a1 = ta[128 * p:128 * p + 64], tb[128 * p:128 * p + 64]
        b0, b1 = roll(ta[128 * p + 64:128 * p + 128], 32), roll(tb[128 * p + 64:128 * p + 128], 32)
        r = (a0, jnp.where(lane64 < 32, a1, b0), jnp.where(lane64 < 32, b0, b1))
        put_raw(0, p, r)
        rs.append(r)
    put_edges(0, rs)

    pl.semaphore_wait(
        barrier, 2 + 3 * has_south.astype(jnp.int32) + 3 * has_north.astype(jnp.int32)
    )
    send(0)

    loads[1].wait()
    for i in range(2):
        for t in range(4):
            tiles = []
            for jl in (2 * t, 2 * t + 1):
                tiles.append(state_in[i, jl].astype(F32))
                tiles.append(state_in[i, jl + 8].astype(F32))
            rows = jnp.concatenate(tiles, axis=0).astype(BF16)
            for c in range(8):
                states[c, 64 * i + 16 * t:64 * i + 16 * t + 16] = rows[:, 128 * c:128 * (c + 1)]
    loads[2].wait()
    loads[3].wait()

    bands = [rband[i] for i in range(2)]

    for step in range(STEPS):
        for i in range(2):
            for b in range(8):
                x = jnp.concatenate(
                    [states[cidx[bands[i], k, b], 64 * i:64 * i + 64] for k in range(2)], axis=1
                )
                w = jnp.concatenate(
                    [coup[bands[i], (2 * b + k) * 128:(2 * b + k + 1) * 128] for k in range(2)], axis=1
                )
                pre[i, b] = dot_nt(x, w)
        for p in range(4):
            ext = []
            for k in range(3):
                r = raw[step, p, k].astype(F32)
                before = jnp.concatenate([r[56:60], r[56:60]], axis=0)
                after = jnp.concatenate([r[4:8], r[4:8]], axis=0)
                ext.append(jnp.concatenate([before, r, after], axis=0))
            for k, block in enumerate(windows(*ext, 8)):
                win[5 + 5 * p + k] = block.astype(BF16)

        for d in range(8):
            wait_recv(step, d)

        lane16 = lanes(16)
        row16 = lax.broadcasted_iota(jnp.int32, (16, 128), 0)
        es = [edge_in[step, 3, k].astype(F32) for k in range(3)]
        ws = minus_parts(*es)
        el = [edge_in[step, 2, k].astype(F32) for k in range(3)]
        wl = plus_parts(el[0], el[1])
        minus_mask = (lane16 < 80, lane16 >= 64, lane16 < 16)
        plus_mask = (lane16 >= 112, lane16 < 64, lane16 >= 48)
        for p in range(4):
            for n, k in enumerate((0, 2, 3)):
                part = ws[n] if p == 0 else pltpu.roll(ws[n], 16 - 4 * p, 0)
                at = 5 + 5 * p + k
                old = win[at, 0:16].astype(F32)
                win[at, 0:16] = jnp.where((row16 < 4) & minus_mask[n], part, old).astype(BF16)
            for n, k in enumerate((1, 2, 4)):
                part = wl[n] if p == 3 else pltpu.roll(wl[n], 12 - 4 * p, 0)
                at = 5 + 5 * p + k
                old = win[at, 48:64].astype(F32)
                win[at, 48:64] = jnp.where((row16 >= 12) & plus_mask[n], part, old).astype(BF16)

        for side, (p, dw, de) in enumerate(((3, 7, 6), (0, 5, 4))):
            ext = []
            for k in range(3):
                r = halo[step, side, k].astype(F32)
                from_west = edge_in[step, dw, k].astype(F32)[4 * p:4 * p + 4]
                from_east = edge_in[step, de, k].astype(F32)[4 * p:4 * p + 4]
                ext.append(jnp.concatenate([from_west, r[56:60], r, r[4:8], from_east], axis=0))
            for k, block in enumerate(windows(*ext, 8)):
                win[25 * side + k] = block.astype(BF16)

        for i in range(2):
            for b in range(8):
                x = win[10 * i + qidx[bands[i], b]]
                w = drive[bands[i], 128 * b:128 * (b + 1)]
                new = jnp.tanh(pre[i, b] + dot_nt(x, w))
                states[b, 64 * i:64 * i + 64] = new.astype(BF16)
                if step == STEPS - 1:
                    for jl in range(8):
                        state_out[i, jl, :, 128 * b:128 * (b + 1)] = new[8 * jl:8 * jl + 4].astype(BF16)
                        state_out[i, jl + 8, :, 128 * b:128 * (b + 1)] = new[8 * jl + 4:8 * jl + 8].astype(BF16)
        if step == 0:
            loads[4].wait()
        x = jnp.concatenate([states[c] for c in range(8)], axis=1)
        if step < STEPS - 1:
            rs = [None] * 4
            for h in range(2):
                y = dot_nt(x, read[0, 320 * h:320 * h + 320])
                y = jnp.concatenate([y, jnp.zeros((128, 64), F32)], axis=1)
                for i in range(2):
                    r = tuple(y[64 * i:64 * i + 64, 128 * k:128 * (k + 1)] for k in range(3))
                    put_raw(step + 1, 2 * i + h, r)
                    rs[2 * i + h] = r
            put_edges(step + 1, rs)
            send(step + 1)
        else:
            for dy in range(4):
                y = dot_nt(x, read[0, 160 * dy:160 * dy + 160])
                for i in range(2):
                    at = 64 * (4 * i + dy)
                    ta[at:at + 64] = y[64 * i:64 * i + 64, 0:128]
                    tb[at:at + 64, 0:32] = y[64 * i:64 * i + 64, 128:160]

    for m in range(4):
        cols = []
        prev = None
        for j in range(16):
            off = (160 * j) % 128
            row = (j % 8) * 8 + (j // 8) * 4 + m
            v0 = ta[pl.ds(row, 8, stride=64), :]
            v1 = tb[pl.ds(row, 8, stride=64), :]
            if off == 0:
                cols.append(v0)
                prev = (v0, v1, 0)
                continue
            r0, r1 = roll(v0, off), roll(v1, off)
            p0, p1, po = prev
            cols.append(jnp.where(lane8 < po, p0, jnp.where(lane8 < po + 32, p1, r0)))
            prev = (r0, r1, off)
            if off == 96:
                cols.append(jnp.where(lane8 < 96, r0, r1))
        for k in range(20):
            field_out[m, :, 128 * k:128 * (k + 1)] = cols[k].astype(BF16)

    for step in range(STEPS):
        by_side(lambda d: message(step, d).wait_send())


def per_device(field_state, reservoir_state, coupling_blocks, coupling_index, input_blocks, input_index, readout, region_band):
    smem = pl.BlockSpec(memory_space=pltpu.SMEM)
    hbm = pl.BlockSpec(memory_space=pl.ANY)
    vmem = pl.BlockSpec(memory_space=pltpu.VMEM)
    return pl.pallas_call(
        kernel,
        out_shape=(
            jax.ShapeDtypeStruct(field_state.shape, BF16),
            jax.ShapeDtypeStruct(reservoir_state.shape, BF16),
        ),
        in_specs=[smem] * 3 + [hbm] * 5,
        out_specs=(vmem, vmem),
        scratch_shapes=[
            pltpu.VMEM(field_state.shape, BF16),
            pltpu.VMEM(reservoir_state.shape, BF16),
            pltpu.VMEM(coupling_blocks.shape, BF16),
            pltpu.VMEM(input_blocks.shape, BF16),
            pltpu.VMEM(readout.shape, BF16),
            pltpu.VMEM((8, 128, 128), BF16),
            pltpu.VMEM((2, 8, 64, 128), F32),
            pltpu.VMEM((30, 64, 128), BF16),
            pltpu.VMEM((STEPS, 4, 3, 64, 128), BF16),
            pltpu.VMEM((STEPS, 2, 3, 64, 128), BF16),
            pltpu.VMEM((STEPS, 2, 3, 16, 128), BF16),
            pltpu.VMEM((STEPS, 8, 3, 16, 128), BF16),
            pltpu.VMEM((512, 128), F32),
            pltpu.VMEM((512, 128), F32),
            pltpu.SemaphoreType.DMA((5,)),
            pltpu.SemaphoreType.DMA((STEPS, 8)),
            pltpu.SemaphoreType.DMA((STEPS, 8)),
        ],
        compiler_params=pltpu.CompilerParams(
            collective_id=0, has_side_effects=True, vmem_limit_bytes=60 * 1024 * 1024
        ),
        name="forecast",
    )(
        jnp.swapaxes(coupling_index, 1, 2), input_index, region_band,
        field_state, reservoir_state, coupling_blocks, input_blocks, readout,
    )


def solution(mesh):
    return jax.shard_map(
        per_device,
        mesh=mesh,
        in_specs=(
            P(None, "lat", "lon"),
            P("lat", "lon", None, None),
            P("lat", None, None),
            P("lat", None, None),
            P("lat", None, None),
            P("lat", None),
            P("lat", None, None),
            P("lat"),
        ),
        out_specs=(P(None, "lat", "lon"), P("lat", "lon", None, None)),
        check_vma=False,
    )
```

```python
import functools

import jax
import jax.numpy as jnp
from jax import lax
from jax.experimental import pallas as pl
from jax.experimental.pallas import tpu as pltpu
from jax.sharding import PartitionSpec as P

MESH = pl.DeviceIdType.MESH
STEPS = 3
F32 = jnp.float32
BF16 = jnp.bfloat16

DIRS = ((-1, 0), (1, 0), (0, -1), (0, 1), (-1, -1), (-1, 1), (1, -1), (1, 1))


def dot_nt(x, w):
    return lax.dot_general(x, w, (((1,), (1,)), ((), ())), preferred_element_type=F32)


def lanes(rows):
    return lax.broadcasted_iota(jnp.int32, (rows, 128), 1)


def roll(x, by):
    return pltpu.roll(x, by, 1)


def minus_parts(r0, r1, r2):
    lane = lanes(r0.shape[0])
    b0 = jnp.where(lane < 48, roll(r0, 48), roll(r1, 48))
    r2r = roll(r2, 80)
    b2 = jnp.where(lane < 80, roll(r1, 80), r2r)
    return b0, b2, r2r


def plus_parts(r0, r1):
    r0r = roll(r0, 112)
    return r0r, r0r, roll(r1, 16)


def windows(r0, r1, r2, n):
    rows = 8 * n
    lane = lanes(rows)
    m = slice(0, rows)
    c = slice(8, rows + 8)
    p = slice(16, rows + 16)
    m0, m2, m3 = minus_parts(r0[m], r1[m], r2[m])
    p1, p2, p4 = plus_parts(r0[p], r1[p])
    c0 = roll(r0[c], 80)
    c1 = roll(r1[c], 80)
    d1 = roll(r1[c], 112)
    d2 = roll(r2[c], 112)
    b0 = jnp.where(lane < 80, m0, c0)
    b1 = jnp.where(lane < 80, c0, jnp.where(lane < 112, c1, p1))
    b2 = jnp.where(lane < 64, p2, m2)
    b3 = jnp.where(lane < 16, m3, jnp.where(lane < 112, d1, d2))
    b4 = jnp.where(lane < 48, d2, p4)
    return b0, b1, b2, b3, b4


def kernel(
    cidx_hbm, qidx_hbm, rband_hbm,
    field_hbm, state_hbm, coup_hbm, drive_hbm, read_hbm,
    field_out, state_out,
    cidx, qidx, rband,
    field_in, state_in, coup, drive, read,
    states, pre, win, raw, halo, edge, edge_in, ta, tb,
    local_sem, send_sem, recv_sem,
):
    lat, lon = lax.axis_index("lat"), lax.axis_index("lon")
    nlat, nlon = lax.axis_size("lat"), lax.axis_size("lon")
    west, east = lax.rem(lon + nlon - 1, nlon), lax.rem(lon + 1, nlon)
    has_south = lat > 0
    has_north = lat < nlat - 1

    def target(d):
        dl, do = DIRS[d]
        return (lat + dl, west if do < 0 else (east if do > 0 else lon))

    def by_side(fn):
        for d in (0, 4, 5, 1, 6, 7, 2, 3):
            dl = DIRS[d][0]
            if dl == 0:
                fn(d)
            else:
                pl.when(has_south if dl < 0 else has_north)(functools.partial(fn, d))

    barrier = pltpu.get_barrier_semaphore()
    by_side(lambda d: pl.semaphore_signal(barrier, inc=1, device_id=target(d), device_id_type=MESH))

    loads = [
        pltpu.make_async_copy(src, dst, local_sem.at[n])
        for n, (src, dst) in enumerate(
            ((field_hbm, field_in), (state_hbm, state_in), (coup_hbm, coup), (drive_hbm, drive), (read_hbm, read),
             (cidx_hbm, cidx), (qidx_hbm, qidx), (rband_hbm, rband))
        )
    ]
    for load in loads:
        load.start()

    @pl.when(lat == 0)
    def _():
        halo[:, 0] = jnp.zeros(halo.shape[:1] + halo.shape[2:], BF16)
        edge_in[:, 6:8] = jnp.zeros((STEPS, 2) + edge_in.shape[2:], BF16)

    @pl.when(lat == nlat - 1)
    def _():
        halo[:, 1] = jnp.zeros(halo.shape[:1] + halo.shape[2:], BF16)
        edge_in[:, 4:6] = jnp.zeros((STEPS, 2) + edge_in.shape[2:], BF16)

    def message(step, d):
        if d == 0:
            src, dst = raw.at[step, 0], halo.at[step, 1]
        elif d == 1:
            src, dst = raw.at[step, 3], halo.at[step, 0]
        else:
            src, dst = edge.at[step, 0 if DIRS[d][1] < 0 else 1], edge_in.at[step, d]
        return pltpu.make_async_remote_copy(
            src_ref=src, dst_ref=dst, send_sem=send_sem.at[step, d], recv_sem=recv_sem.at[step, d],
            device_id=target(d), device_id_type=MESH,
        )

    def wait_recv(step, d):
        dl = DIRS[d][0]
        if dl == 0:
            message(step, d).wait_recv()
        else:
            @pl.when(has_north if dl < 0 else has_south)
            def _():
                message(step, d).wait_recv()

    def put_raw(step, pair, r):
        for k in range(3):
            raw[step, pair, k] = r[k].astype(BF16)

    def put_edges(step, rs):
        for k in range(3):
            first = jnp.concatenate([rs[p][k][0:4] for p in range(4)], axis=0)
            last = jnp.concatenate([rs[p][k][60:64] for p in range(4)], axis=0)
            edge[step, 0, k] = first.astype(BF16)
            edge[step, 1, k] = last.astype(BF16)

    def send(step):
        by_side(lambda d: message(step, d).start())

    loads[0].wait()
    lane8 = lanes(8)
    for m in range(4):
        f = [field_in[m, :, 128 * k:128 * (k + 1)].astype(F32) for k in range(20)]
        for j in range(16):
            q, off = (160 * j) // 128, (160 * j) % 128
            row = (j % 8) * 8 + (j // 8) * 4 + m
            if off == 0:
                w0, w1 = f[q], f[q + 1]
            else:
                w1 = roll(f[q + 1], 128 - off)
                w0 = jnp.where(lane8 < 128 - off, roll(f[q], 128 - off), w1)
            ta[pl.ds(row, 8, stride=64), :] = w0
            tb[pl.ds(row, 8, stride=64), :] = w1
    lane64 = lanes(64)
    rs = []
    for p in range(4):
        a0, a1 = ta[128 * p:128 * p + 64], tb[128 * p:128 * p + 64]
        b0, b1 = roll(ta[128 * p + 64:128 * p + 128], 32), roll(tb[128 * p + 64:128 * p + 128], 32)
        r = (a0, jnp.where(lane64 < 32, a1, b0), jnp.where(lane64 < 32, b0, b1))
        put_raw(0, p, r)
        rs.append(r)
    put_edges(0, rs)

    pl.semaphore_wait(
        barrier, 2 + 3 * has_south.astype(jnp.int32) + 3 * has_north.astype(jnp.int32)
    )
    send(0)

    loads[1].wait()
    for i in range(2):
        for t in range(4):
            tiles = []
            for jl in (2 * t, 2 * t + 1):
                tiles.append(state_in[i, jl].astype(F32))
                tiles.append(state_in[i, jl + 8].astype(F32))
            rows = jnp.concatenate(tiles, axis=0).astype(BF16)
            for c in range(8):
                states[c, 64 * i + 16 * t:64 * i + 16 * t + 16] = rows[:, 128 * c:128 * (c + 1)]
    loads[2].wait()
    loads[3].wait()

    for load in loads[5:]:
        load.wait()
    bands = [rband[i] for i in range(2)]

    for step in range(STEPS):
        for i in range(2):
            for b in range(8):
                x = jnp.concatenate(
                    [states[cidx[bands[i], k, b], 64 * i:64 * i + 64] for k in range(2)], axis=1
                )
                w = jnp.concatenate(
                    [coup[bands[i], (2 * b + k) * 128:(2 * b + k + 1) * 128] for k in range(2)], axis=1
                )
                pre[i, b] = dot_nt(x, w)
        for p in range(4):
            ext = []
            for k in range(3):
                r = raw[step, p, k].astype(F32)
                before = jnp.concatenate([r[56:60], r[56:60]], axis=0)
                after = jnp.concatenate([r[4:8], r[4:8]], axis=0)
                ext.append(jnp.concatenate([before, r, after], axis=0))
            for k, block in enumerate(windows(*ext, 8)):
                win[5 + 5 * p + k] = block.astype(BF16)

        for d in range(8):
            wait_recv(step, d)

        lane16 = lanes(16)
        row16 = lax.broadcasted_iota(jnp.int32, (16, 128), 0)
        es = [edge_in[step, 3, k].astype(F32) for k in range(3)]
        ws = minus_parts(*es)
        el = [edge_in[step, 2, k].astype(F32) for k in range(3)]
        wl = plus_parts(el[0], el[1])
        minus_mask = (lane16 < 80, lane16 >= 64, lane16 < 16)
        plus_mask = (lane16 >= 112, lane16 < 64, lane16 >= 48)
        for p in range(4):
            for n, k in enumerate((0, 2, 3)):
                part = ws[n] if p == 0 else pltpu.roll(ws[n], 16 - 4 * p, 0)
                at = 5 + 5 * p + k
                old = win[at, 0:16].astype(F32)
                win[at, 0:16] = jnp.where((row16 < 4) & minus_mask[n], part, old).astype(BF16)
            for n, k in enumerate((1, 2, 4)):
                part = wl[n] if p == 3 else pltpu.roll(wl[n], 12 - 4 * p, 0)
                at = 5 + 5 * p + k
                old = win[at, 48:64].astype(F32)
                win[at, 48:64] = jnp.where((row16 >= 12) & plus_mask[n], part, old).astype(BF16)

        for side, (p, dw, de) in enumerate(((3, 7, 6), (0, 5, 4))):
            ext = []
            for k in range(3):
                r = halo[step, side, k].astype(F32)
                from_west = edge_in[step, dw, k].astype(F32)[4 * p:4 * p + 4]
                from_east = edge_in[step, de, k].astype(F32)[4 * p:4 * p + 4]
                ext.append(jnp.concatenate([from_west, r[56:60], r, r[4:8], from_east], axis=0))
            for k, block in enumerate(windows(*ext, 8)):
                win[25 * side + k] = block.astype(BF16)

        for i in range(2):
            for b in range(8):
                x = win[10 * i + qidx[bands[i], b]]
                w = drive[bands[i], 128 * b:128 * (b + 1)]
                new = jnp.tanh(pre[i, b] + dot_nt(x, w))
                states[b, 64 * i:64 * i + 64] = new.astype(BF16)
                if step == STEPS - 1:
                    for jl in range(8):
                        state_out[i, jl, :, 128 * b:128 * (b + 1)] = new[8 * jl:8 * jl + 4].astype(BF16)
                        state_out[i, jl + 8, :, 128 * b:128 * (b + 1)] = new[8 * jl + 4:8 * jl + 8].astype(BF16)
        if step == 0:
            loads[4].wait()
        x = jnp.concatenate([states[c] for c in range(8)], axis=1)
        if step < STEPS - 1:
            rs = [None] * 4
            for h in range(2):
                y = dot_nt(x, read[0, 320 * h:320 * h + 320])
                y = jnp.concatenate([y, jnp.zeros((128, 64), F32)], axis=1)
                for i in range(2):
                    r = tuple(y[64 * i:64 * i + 64, 128 * k:128 * (k + 1)] for k in range(3))
                    put_raw(step + 1, 2 * i + h, r)
                    rs[2 * i + h] = r
            put_edges(step + 1, rs)
            send(step + 1)
        else:
            for dy in range(4):
                y = dot_nt(x, read[0, 160 * dy:160 * dy + 160])
                for i in range(2):
                    at = 64 * (4 * i + dy)
                    ta[at:at + 64] = y[64 * i:64 * i + 64, 0:128]
                    tb[at:at + 64, 0:32] = y[64 * i:64 * i + 64, 128:160]

    for m in range(4):
        cols = []
        prev = None
        for j in range(16):
            off = (160 * j) % 128
            row = (j % 8) * 8 + (j // 8) * 4 + m
            v0 = ta[pl.ds(row, 8, stride=64), :]
            v1 = tb[pl.ds(row, 8, stride=64), :]
            if off == 0:
                cols.append(v0)
                prev = (v0, v1, 0)
                continue
            r0, r1 = roll(v0, off), roll(v1, off)
            p0, p1, po = prev
            cols.append(jnp.where(lane8 < po, p0, jnp.where(lane8 < po + 32, p1, r0)))
            prev = (r0, r1, off)
            if off == 96:
                cols.append(jnp.where(lane8 < 96, r0, r1))
        for k in range(20):
            field_out[m, :, 128 * k:128 * (k + 1)] = cols[k].astype(BF16)

    for step in range(STEPS):
        by_side(lambda d: message(step, d).wait_send())


def deliver(field_ref, state_ref, field_out, state_out, sems):
    copies = [
        pltpu.make_async_copy(field_ref, field_out, sems.at[0]),
        pltpu.make_async_copy(state_ref, state_out, sems.at[1]),
    ]
    for copy in copies:
        copy.start()
    for copy in copies:
        copy.wait()


def per_device(field_state, reservoir_state, coupling_blocks, coupling_index, input_blocks, input_index, readout, region_band):
    hbm = pl.BlockSpec(memory_space=pltpu.HBM)
    vmem = pl.BlockSpec(memory_space=pltpu.VMEM)
    field, state = pl.pallas_call(
        kernel,
        out_shape=(
            pltpu.VMEM(field_state.shape, BF16),
            pltpu.VMEM(reservoir_state.shape, BF16),
        ),
        in_specs=[hbm] * 8,
        out_specs=(vmem, vmem),
        scratch_shapes=[
            pltpu.SMEM((2, 2, 8), jnp.int32),
            pltpu.SMEM((2, 8), jnp.int32),
            pltpu.SMEM((2,), jnp.int32),
            pltpu.VMEM(field_state.shape, BF16),
            pltpu.VMEM(reservoir_state.shape, BF16),
            pltpu.VMEM(coupling_blocks.shape, BF16),
            pltpu.VMEM(input_blocks.shape, BF16),
            pltpu.VMEM(readout.shape, BF16),
            pltpu.VMEM((8, 128, 128), BF16),
            pltpu.VMEM((2, 8, 64, 128), F32),
            pltpu.VMEM((30, 64, 128), BF16),
            pltpu.VMEM((STEPS, 4, 3, 64, 128), BF16),
            pltpu.VMEM((STEPS, 2, 3, 64, 128), BF16),
            pltpu.VMEM((STEPS, 2, 3, 16, 128), BF16),
            pltpu.VMEM((STEPS, 8, 3, 16, 128), BF16),
            pltpu.VMEM((512, 128), F32),
            pltpu.VMEM((512, 128), F32),
            pltpu.SemaphoreType.DMA((8,)),
            pltpu.SemaphoreType.DMA((STEPS, 8)),
            pltpu.SemaphoreType.DMA((STEPS, 8)),
        ],
        compiler_params=pltpu.CompilerParams(
            collective_id=0, has_side_effects=True, vmem_limit_bytes=32 * 1024 * 1024
        ),
        name="forecast",
    )(
        *(
            pltpu.with_memory_space_constraint(x, pltpu.HBM)
            for x in (
                jnp.swapaxes(coupling_index, 1, 2), input_index, region_band,
                field_state, reservoir_state, coupling_blocks, input_blocks, readout,
            )
        )
    )
    return pl.pallas_call(
        deliver,
        out_shape=(
            jax.ShapeDtypeStruct(field_state.shape, BF16),
            jax.ShapeDtypeStruct(reservoir_state.shape, BF16),
        ),
        in_specs=[vmem] * 2,
        out_specs=(hbm, hbm),
        scratch_shapes=[pltpu.SemaphoreType.DMA((2,))],
        compiler_params=pltpu.CompilerParams(vmem_limit_bytes=32 * 1024 * 1024),
        name="deliver",
    )(*(pltpu.with_memory_space_constraint(x, pltpu.VMEM) for x in (field, state)))


def solution(mesh):
    return jax.shard_map(
        per_device,
        mesh=mesh,
        in_specs=(
            P(None, "lat", "lon"),
            P("lat", "lon", None, None),
            P("lat", None, None),
            P("lat", None, None),
            P("lat", None, None),
            P("lat", None),
            P("lat", None, None),
            P("lat"),
        ),
        out_specs=(P(None, "lat", "lon"), P("lat", "lon", None, None)),
        check_vma=False,
    )
```

```python
import functools

import jax
import jax.numpy as jnp
from jax import lax
from jax.experimental import pallas as pl
from jax.experimental.pallas import tpu as pltpu
from jax.sharding import PartitionSpec as P

MESH = pl.DeviceIdType.MESH
STEPS = 3
F32 = jnp.float32
BF16 = jnp.bfloat16
TILES = 10
ROWS = 8 * TILES

DIRS = ((-1, 0), (1, 0), (0, -1), (0, 1), (-1, -1), (-1, 1), (1, -1), (1, 1))


def dot_nt(x, w):
    return lax.dot_general(x, w, (((1,), (1,)), ((), ())), preferred_element_type=F32)


def row_of(column, member):
    at = column + 2
    return at % TILES * 8 + at // TILES * 4 + member


def lanes(rows):
    return lax.broadcasted_iota(jnp.int32, (rows, 128), 1)


def roll(x, by):
    return pltpu.roll(x, by, 1)


def minus_parts(r0, r1, r2):
    lane = lanes(r0.shape[0])
    b0 = jnp.where(lane < 48, roll(r0, 48), roll(r1, 48))
    r2r = roll(r2, 80)
    b2 = jnp.where(lane < 80, roll(r1, 80), r2r)
    return b0, b2, r2r


def plus_parts(r0, r1):
    r0r = roll(r0, 112)
    return r0r, r0r, roll(r1, 16)


def windows(r0, r1, r2, n):
    rows = 8 * n
    lane = lanes(rows)
    m = slice(0, rows)
    c = slice(8, rows + 8)
    p = slice(16, rows + 16)
    m0, m2, m3 = minus_parts(r0[m], r1[m], r2[m])
    p1, p2, p4 = plus_parts(r0[p], r1[p])
    c0 = roll(r0[c], 80)
    c1 = roll(r1[c], 80)
    d1 = roll(r1[c], 112)
    d2 = roll(r2[c], 112)
    b0 = jnp.where(lane < 80, m0, c0)
    b1 = jnp.where(lane < 80, c0, jnp.where(lane < 112, c1, p1))
    b2 = jnp.where(lane < 64, p2, m2)
    b3 = jnp.where(lane < 16, m3, jnp.where(lane < 112, d1, d2))
    b4 = jnp.where(lane < 48, d2, p4)
    return b0, b1, b2, b3, b4


def kernel(
    cidx_hbm, qidx_hbm, rband_hbm,
    field_hbm, state_hbm, coup_hbm, drive_hbm, read_hbm,
    field_out, state_out,
    cidx, qidx, rband,
    field_in, state_in, coup, drive, read,
    states, pre, win, raw, halo, edge, edge_in, state_edge, ta, tb,
    local_sem, send_sem, recv_sem,
):
    lat, lon = lax.axis_index("lat"), lax.axis_index("lon")
    nlat, nlon = lax.axis_size("lat"), lax.axis_size("lon")
    west, east = lax.rem(lon + nlon - 1, nlon), lax.rem(lon + 1, nlon)
    has_south = lat > 0
    has_north = lat < nlat - 1

    def target(d):
        dl, do = DIRS[d]
        return (lat + dl, west if do < 0 else (east if do > 0 else lon))

    def by_side(fn, dirs=range(8)):
        for d in dirs:
            dl = DIRS[d][0]
            if dl == 0:
                fn(d)
            else:
                pl.when(has_south if dl < 0 else has_north)(functools.partial(fn, d))

    barrier = pltpu.get_barrier_semaphore()
    by_side(
        lambda d: pl.semaphore_signal(barrier, inc=1, device_id=target(d), device_id_type=MESH),
        (4, 5, 6, 7, 2, 3, 0, 1),
    )

    loads = [
        pltpu.make_async_copy(src, dst, local_sem.at[n])
        for n, (src, dst) in enumerate(
            ((field_hbm, field_in), (state_hbm, state_in), (coup_hbm, coup), (drive_hbm, drive), (read_hbm, read),
             (cidx_hbm, cidx), (qidx_hbm, qidx), (rband_hbm, rband))
        )
    ]
    for load in loads:
        load.start()

    @pl.when(lat == 0)
    def _():
        halo[:, 0] = jnp.zeros(halo.shape[:1] + halo.shape[2:], BF16)
        edge_in[2:4, 3] = jnp.zeros((2,) + edge_in.shape[2:], BF16)

    @pl.when(lat == nlat - 1)
    def _():
        halo[:, 1] = jnp.zeros(halo.shape[:1] + halo.shape[2:], BF16)
        edge_in[2:4, 0] = jnp.zeros((2,) + edge_in.shape[2:], BF16)

    def remote(src, dst, step, n, d):
        return pltpu.make_async_remote_copy(
            src_ref=src, dst_ref=dst, send_sem=send_sem.at[step, n], recv_sem=recv_sem.at[step, n],
            device_id=target(d), device_id_type=MESH,
        )

    def message(step, d):
        if d == 0:
            return remote(raw.at[step, 0], halo.at[step, 1], step, d, d)
        if d == 1:
            return remote(raw.at[step, 3], halo.at[step, 0], step, d, d)
        dl, do = DIRS[d]
        side, into = (0, 1) if do < 0 else (1, 0)
        if dl == 0:
            return remote(edge.at[side], edge_in.at[into], step, d, d)
        pair = 0 if dl < 0 else 3
        return remote(edge.at[side, pair], edge_in.at[2 + into, pair], step, d, d)

    def state_message(d):
        side, into = (0, 1) if DIRS[d][1] < 0 else (1, 0)
        return remote(state_hbm.at[:, pl.ds(14 * side, 2)], state_edge.at[into], 0, 6 + d, d)

    def wait_recv(step, dirs):
        for d in dirs:
            dl = DIRS[d][0]
            if dl == 0:
                message(step, d).wait_recv()
            else:
                pl.when(has_north if dl < 0 else has_south)(message(step, d).wait_recv)

    def put_raw(step, pair, r):
        for k in range(3):
            raw[step, pair, k] = r[k].astype(BF16)

    loads[0].wait()
    lane8 = lanes(8)
    for m in range(4):
        f = [field_in[m, :, 128 * k:128 * (k + 1)].astype(F32) for k in range(20)]
        for j in range(16):
            q, off = (160 * j) // 128, (160 * j) % 128
            if off == 0:
                w0, w1 = f[q], f[q + 1]
            else:
                w1 = roll(f[q + 1], 128 - off)
                w0 = jnp.where(lane8 < 128 - off, roll(f[q], 128 - off), w1)
            ta[pl.ds(row_of(j, m), 8, stride=ROWS), :] = w0
            tb[pl.ds(row_of(j, m), 8, stride=ROWS), :] = w1
    lane_all = lanes(ROWS)
    for p in range(4):
        lo, mid, hi = 2 * p * ROWS, (2 * p + 1) * ROWS, (2 * p + 2) * ROWS
        a0, a1 = ta[lo:mid], tb[lo:mid]
        b0, b1 = roll(ta[mid:hi], 32), roll(tb[mid:hi], 32)
        r = (a0, jnp.where(lane_all < 32, a1, b0), jnp.where(lane_all < 32, b0, b1))
        put_raw(0, p, r)
        for k in range(3):
            for side, cols in enumerate(((0, 1, 2), (13, 14, 15))):
                at = [row_of(j, 0) for j in cols]
                at.append(at[0])
                rows = jnp.concatenate([r[k][x:x + 4] for x in at], axis=0)
                edge[side, p, k] = rows.astype(BF16)

    pl.semaphore_wait(
        barrier, 2 + 3 * has_south.astype(jnp.int32) + 3 * has_north.astype(jnp.int32)
    )
    by_side(lambda d: message(0, d).start(), (4, 5, 6, 7, 2, 3))
    for d in (2, 3):
        state_message(d).start()
    by_side(lambda d: message(0, d).start(), (0, 1))

    def put_state(i, t):
        tiles = []
        for s in (t, t + 1):
            tiles.append(state_in[i, s - 2] if s >= 2 else state_edge[0, i, s])
            tiles.append(state_in[i, s + 8] if s < 8 else state_edge[1, i, s - 8])
        rows = jnp.concatenate([x.astype(F32) for x in tiles], axis=0).astype(BF16)
        for c in range(8):
            states[c, ROWS * i + 8 * t:ROWS * i + 8 * t + 16] = rows[:, 128 * c:128 * (c + 1)]

    loads[1].wait()
    for i in range(2):
        for t in (2, 4, 6):
            put_state(i, t)
    for load in loads[2:4] + loads[5:]:
        load.wait()
    bands = [rband[i] for i in range(2)]

    def put_windows(at, ext):
        for k, block in enumerate(windows(*ext, TILES)):
            win[at + k] = block.astype(BF16)

    def with_edges(r, w, x):
        return jnp.concatenate(
            [
                w[0:4], r[72:76], w[4:8], r[4:8], w[8:12], r[12:16],
                r[16:64],
                r[64:68], x[0:4], r[72:76], x[4:8], r[4:8], x[8:12],
            ],
            axis=0,
        )

    def without_edges(r):
        return jnp.concatenate([r[72:76], r[72:76], r, r[4:8], r[4:8]], axis=0)

    for step in range(STEPS):
        if step == 0:
            for d in (2, 3):
                state_message(d).wait_recv()
            for i in range(2):
                for t in (0, 8):
                    put_state(i, t)
        for i in range(2):
            for b in range(8):
                x = jnp.concatenate(
                    [states[cidx[bands[i], k, b], ROWS * i:ROWS * (i + 1)] for k in range(2)], axis=1
                )
                w = jnp.concatenate(
                    [coup[bands[i], (2 * b + k) * 128:(2 * b + k + 1) * 128] for k in range(2)], axis=1
                )
                pre[i, b] = dot_nt(x, w)
        if step == 0:
            wait_recv(step, (2, 3))
        for p in range(4):
            ext = []
            for k in range(3):
                r = raw[step, p, k].astype(F32)
                if step == 0:
                    w, x = (edge_in[side, p, k].astype(F32) for side in range(2))
                    ext.append(with_edges(r, w, x))
                else:
                    ext.append(without_edges(r))
            put_windows(5 + 5 * p, ext)

        wait_recv(step, (0, 1) + ((4, 5, 6, 7) if step == 0 else ()))
        for side, p in enumerate((3, 0)):
            ext = []
            for k in range(3):
                r = halo[step, side, k].astype(F32)
                if step == 0:
                    w, x = (edge_in[2 + s, p, k].astype(F32) for s in range(2))
                    ext.append(with_edges(r, w, x))
                else:
                    ext.append(without_edges(r))
            put_windows(25 * side, ext)

        for i in range(2):
            for b in range(8):
                x = win[10 * i + qidx[bands[i], b]]
                w = drive[bands[i], 128 * b:128 * (b + 1)]
                new = jnp.tanh(pre[i, b] + dot_nt(x, w))
                states[b, ROWS * i:ROWS * (i + 1)] = new.astype(BF16)
                if step == STEPS - 1:
                    for j in range(16):
                        at = row_of(j, 0)
                        state_out[i, j, :, 128 * b:128 * (b + 1)] = new[at:at + 4].astype(BF16)
        if step == 0:
            loads[4].wait()
        x = jnp.concatenate([states[c] for c in range(8)], axis=1)
        if step < STEPS - 1:
            for h in range(2):
                y = dot_nt(x, read[0, 320 * h:320 * h + 320])
                y = jnp.concatenate([y, jnp.zeros((2 * ROWS, 64), F32)], axis=1)
                for i in range(2):
                    put_raw(
                        step + 1, 2 * i + h,
                        tuple(y[ROWS * i:ROWS * (i + 1), 128 * k:128 * (k + 1)] for k in range(3)),
                    )
                by_side(lambda d: message(step + 1, d).start(), (h,))
        else:
            for dy in range(4):
                y = dot_nt(x, read[0, 160 * dy:160 * dy + 160])
                for i in range(2):
                    at = ROWS * (4 * i + dy)
                    ta[at:at + ROWS] = y[ROWS * i:ROWS * (i + 1), 0:128]
                    tb[at:at + ROWS, 0:32] = y[ROWS * i:ROWS * (i + 1), 128:160]

    for m in range(4):
        cols = []
        prev = None
        for j in range(16):
            off = (160 * j) % 128
            v0 = ta[pl.ds(row_of(j, m), 8, stride=ROWS), :]
            v1 = tb[pl.ds(row_of(j, m), 8, stride=ROWS), :]
            if off == 0:
                cols.append(v0)
                prev = (v0, v1, 0)
                continue
            r0, r1 = roll(v0, off), roll(v1, off)
            p0, p1, po = prev
            cols.append(jnp.where(lane8 < po, p0, jnp.where(lane8 < po + 32, p1, r0)))
            prev = (r0, r1, off)
            if off == 96:
                cols.append(jnp.where(lane8 < 96, r0, r1))
        for k in range(20):
            field_out[m, :, 128 * k:128 * (k + 1)] = cols[k].astype(BF16)

    by_side(lambda d: message(0, d).wait_send())
    for d in (2, 3):
        state_message(d).wait_send()
    for step in range(1, STEPS):
        by_side(lambda d: message(step, d).wait_send(), (0, 1))


def deliver(field_ref, state_ref, field_out, state_out, sems):
    copies = [
        pltpu.make_async_copy(field_ref, field_out, sems.at[0]),
        pltpu.make_async_copy(state_ref, state_out, sems.at[1]),
    ]
    for copy in copies:
        copy.start()
    for copy in copies:
        copy.wait()


def per_device(field_state, reservoir_state, coupling_blocks, coupling_index, input_blocks, input_index, readout, region_band):
    hbm = pl.BlockSpec(memory_space=pltpu.HBM)
    vmem = pl.BlockSpec(memory_space=pltpu.VMEM)
    field, state = pl.pallas_call(
        kernel,
        out_shape=(
            pltpu.VMEM(field_state.shape, BF16),
            pltpu.VMEM(reservoir_state.shape, BF16),
        ),
        in_specs=[hbm] * 8,
        out_specs=(vmem, vmem),
        scratch_shapes=[
            pltpu.SMEM((2, 2, 8), jnp.int32),
            pltpu.SMEM((2, 8), jnp.int32),
            pltpu.SMEM((2,), jnp.int32),
            pltpu.VMEM(field_state.shape, BF16),
            pltpu.VMEM(reservoir_state.shape, BF16),
            pltpu.VMEM(coupling_blocks.shape, BF16),
            pltpu.VMEM(input_blocks.shape, BF16),
            pltpu.VMEM(readout.shape, BF16),
            pltpu.VMEM((8, 2 * ROWS, 128), BF16),
            pltpu.VMEM((2, 8, ROWS, 128), F32),
            pltpu.VMEM((30, ROWS, 128), BF16),
            pltpu.VMEM((STEPS, 4, 3, ROWS, 128), BF16),
            pltpu.VMEM((STEPS, 2, 3, ROWS, 128), BF16),
            pltpu.VMEM((2, 4, 3, 16, 128), BF16),
            pltpu.VMEM((4, 4, 3, 16, 128), BF16),
            pltpu.VMEM((2, 2, 2, 4, 1024), BF16),
            pltpu.VMEM((8 * ROWS, 128), F32),
            pltpu.VMEM((8 * ROWS, 128), F32),
            pltpu.SemaphoreType.DMA((8,)),
            pltpu.SemaphoreType.DMA((STEPS, 10)),
            pltpu.SemaphoreType.DMA((STEPS, 10)),
        ],
        compiler_params=pltpu.CompilerParams(
            collective_id=0, has_side_effects=True, vmem_limit_bytes=32 * 1024 * 1024
        ),
        name="forecast",
    )(
        *(
            pltpu.with_memory_space_constraint(x, pltpu.HBM)
            for x in (
                jnp.swapaxes(coupling_index, 1, 2), input_index, region_band,
                field_state, reservoir_state, coupling_blocks, input_blocks, readout,
            )
        )
    )
    return pl.pallas_call(
        deliver,
        out_shape=(
            jax.ShapeDtypeStruct(field_state.shape, BF16),
            jax.ShapeDtypeStruct(reservoir_state.shape, BF16),
        ),
        in_specs=[vmem] * 2,
        out_specs=(hbm, hbm),
        scratch_shapes=[pltpu.SemaphoreType.DMA((2,))],
        compiler_params=pltpu.CompilerParams(vmem_limit_bytes=32 * 1024 * 1024),
        name="deliver",
    )(*(pltpu.with_memory_space_constraint(x, pltpu.VMEM) for x in (field, state)))


def solution(mesh):
    return jax.shard_map(
        per_device,
        mesh=mesh,
        in_specs=(
            P(None, "lat", "lon"),
            P("lat", "lon", None, None),
            P("lat", None, None),
            P("lat", None, None),
            P("lat", None, None),
            P("lat", None),
            P("lat", None, None),
            P("lat"),
        ),
        out_specs=(P(None, "lat", "lon"), P("lat", "lon", None, None)),
        check_vma=False,
    )
```

```python
import functools

import jax
import jax.numpy as jnp
from jax import lax
from jax.experimental import pallas as pl
from jax.experimental.pallas import tpu as pltpu
from jax.sharding import PartitionSpec as P

MESH = pl.DeviceIdType.MESH
STEPS = 3
F32 = jnp.float32
BF16 = jnp.bfloat16
TILES = 10
ROWS = 8 * TILES

DIRS = ((-1, 0), (1, 0), (0, -1), (0, 1), (-1, -1), (-1, 1), (1, -1), (1, 1))


def dot_nt(x, w):
    return lax.dot_general(x, w, (((1,), (1,)), ((), ())), preferred_element_type=F32)


def row_of(column, member):
    at = column + 2
    return at % TILES * 8 + at // TILES * 4 + member


def lanes(rows):
    return lax.broadcasted_iota(jnp.int32, (rows, 128), 1)


def roll(x, by):
    return pltpu.roll(x, by, 1)


def minus_parts(r0, r1, r2):
    lane = lanes(r0.shape[0])
    b0 = jnp.where(lane < 48, roll(r0, 48), roll(r1, 48))
    r2r = roll(r2, 80)
    b2 = jnp.where(lane < 80, roll(r1, 80), r2r)
    return b0, b2, r2r


def plus_parts(r0, r1):
    r0r = roll(r0, 112)
    return r0r, r0r, roll(r1, 16)


def windows(r0, r1, r2, n):
    rows = 8 * n
    lane = lanes(rows)
    m = slice(0, rows)
    c = slice(8, rows + 8)
    p = slice(16, rows + 16)
    m0, m2, m3 = minus_parts(r0[m], r1[m], r2[m])
    p1, p2, p4 = plus_parts(r0[p], r1[p])
    c0 = roll(r0[c], 80)
    c1 = roll(r1[c], 80)
    d1 = roll(r1[c], 112)
    d2 = roll(r2[c], 112)
    b0 = jnp.where(lane < 80, m0, c0)
    b1 = jnp.where(lane < 80, c0, jnp.where(lane < 112, c1, p1))
    b2 = jnp.where(lane < 64, p2, m2)
    b3 = jnp.where(lane < 16, m3, jnp.where(lane < 112, d1, d2))
    b4 = jnp.where(lane < 48, d2, p4)
    return b0, b1, b2, b3, b4


def kernel(
    cidx_hbm, qidx_hbm, rband_hbm,
    field_hbm, state_hbm, coup_hbm, drive_hbm, read_hbm,
    field_out, state_out,
    cidx, qidx, rband,
    field_in, state_in, coup, drive, read,
    states, pre, win, raw, halo, edge, edge_in, state_edge, ta, tb,
    local_sem, send_sem, recv_sem, ready,
):
    lat, lon = lax.axis_index("lat"), lax.axis_index("lon")
    nlat, nlon = lax.axis_size("lat"), lax.axis_size("lon")
    west, east = lax.rem(lon + nlon - 1, nlon), lax.rem(lon + 1, nlon)
    has_south = lat > 0
    has_north = lat < nlat - 1

    def target(d):
        dl, do = DIRS[d]
        return (lat + dl, west if do < 0 else (east if do > 0 else lon))

    def by_side(fn, dirs=range(8)):
        for d in dirs:
            dl = DIRS[d][0]
            if dl == 0:
                fn(d)
            else:
                pl.when(has_south if dl < 0 else has_north)(functools.partial(fn, d))

    is_first = lon == 0
    is_last = lon == nlon - 1
    is_before_last = lon == nlon - 2
    greeted = 1 + has_south.astype(jnp.int32) + has_north.astype(jnp.int32)

    barrier = pltpu.get_barrier_semaphore()

    def greet(d):
        pl.semaphore_signal(barrier, inc=1, device_id=target(d), device_id_type=MESH)

    by_side(greet, (4, 6, 2))

    @pl.when(jnp.logical_not(is_last))
    def _():
        by_side(greet, (0, 1))
        pl.when(jnp.logical_not(is_before_last))(lambda: by_side(greet, (5, 7, 3)))

    loads = [
        pltpu.make_async_copy(src, dst, local_sem.at[n])
        for n, (src, dst) in enumerate(
            ((field_hbm, field_in), (state_hbm, state_in), (coup_hbm, coup), (drive_hbm, drive), (read_hbm, read),
             (cidx_hbm, cidx), (qidx_hbm, qidx), (rband_hbm, rband))
        )
    ]
    for load in loads:
        load.start()

    @pl.when(lat == 0)
    def _():
        halo[:, 0] = jnp.zeros(halo.shape[:1] + halo.shape[2:], BF16)
        edge_in[2:4, 3] = jnp.zeros((2,) + edge_in.shape[2:], BF16)

    @pl.when(lat == nlat - 1)
    def _():
        halo[:, 1] = jnp.zeros(halo.shape[:1] + halo.shape[2:], BF16)
        edge_in[2:4, 0] = jnp.zeros((2,) + edge_in.shape[2:], BF16)

    def remote(src, dst, step, n, d):
        return pltpu.make_async_remote_copy(
            src_ref=src, dst_ref=dst, send_sem=send_sem.at[step, n], recv_sem=recv_sem.at[step, n],
            device_id=target(d), device_id_type=MESH,
        )

    def message(step, d):
        if d == 0:
            return remote(raw.at[step, 0], halo.at[step, 1], step, d, d)
        if d == 1:
            return remote(raw.at[step, 3], halo.at[step, 0], step, d, d)
        dl, do = DIRS[d]
        side, into = (0, 1) if do < 0 else (1, 0)
        if dl == 0:
            return remote(edge.at[side], edge_in.at[into], step, d, d)
        pair = 0 if dl < 0 else 3
        return remote(edge.at[side, pair], edge_in.at[2 + into, pair], step, d, d)

    def state_message(d):
        side, into = (0, 1) if DIRS[d][1] < 0 else (1, 0)
        return remote(state_hbm.at[:, pl.ds(14 * side, 2)], state_edge.at[into], 0, 6 + d, d)

    def wait_recv(step, dirs):
        for d in dirs:
            dl = DIRS[d][0]
            if dl == 0:
                message(step, d).wait_recv()
            else:
                pl.when(has_north if dl < 0 else has_south)(message(step, d).wait_recv)

    def put_raw(step, pair, r):
        for k in range(3):
            raw[step, pair, k] = r[k].astype(BF16)

    @pl.when(is_last)
    def _():
        pl.semaphore_wait(barrier, greeted)
        state_message(3).start()

    loads[0].wait()
    lane8 = lanes(8)
    for m in range(4):
        f = [field_in[m, :, 128 * k:128 * (k + 1)].astype(F32) for k in range(20)]
        for j in range(16):
            q, off = (160 * j) // 128, (160 * j) % 128
            if off == 0:
                w0, w1 = f[q], f[q + 1]
            else:
                w1 = roll(f[q + 1], 128 - off)
                w0 = jnp.where(lane8 < 128 - off, roll(f[q], 128 - off), w1)
            ta[pl.ds(row_of(j, m), 8, stride=ROWS), :] = w0
            tb[pl.ds(row_of(j, m), 8, stride=ROWS), :] = w1
    lane_all = lanes(ROWS)
    for p in range(4):
        lo, mid, hi = 2 * p * ROWS, (2 * p + 1) * ROWS, (2 * p + 2) * ROWS
        a0, a1 = ta[lo:mid], tb[lo:mid]
        b0, b1 = roll(ta[mid:hi], 32), roll(tb[mid:hi], 32)
        r = (a0, jnp.where(lane_all < 32, a1, b0), jnp.where(lane_all < 32, b0, b1))
        put_raw(0, p, r)
        for k in range(3):
            for side, cols in enumerate(((0, 1, 2), (13, 14, 15))):
                at = [row_of(j, 0) for j in cols]
                at.append(at[0])
                rows = jnp.concatenate([r[k][x:x + 4] for x in at], axis=0)
                edge[side, p, k] = rows.astype(BF16)

    def start(d):
        message(0, d).start()

    def send_west():
        by_side(start, (4, 6, 2))
        state_message(2).start()

    @pl.when(is_last)
    def _():
        by_side(start, (5, 7, 3))
        pl.semaphore_wait(ready, 1)
        by_side(start, (0, 1))
        send_west()

    @pl.when(jnp.logical_not(is_last))
    def _():
        pl.semaphore_wait(barrier, 2 * greeted - 1 + jnp.where(is_first, 0, greeted))

        @pl.when(is_before_last)
        def _():
            pl.semaphore_signal(ready, inc=1, device_id=(lat, east), device_id_type=MESH)

        by_side(start, (5, 7, 3))
        state_message(3).start()
        by_side(start, (0, 1))
        pl.when(jnp.logical_not(is_first))(send_west)

    def put_state(i, t):
        tiles = []
        for s in (t, t + 1):
            tiles.append(state_in[i, s - 2] if s >= 2 else state_edge[0, i, s])
            tiles.append(state_in[i, s + 8] if s < 8 else state_edge[1, i, s - 8])
        rows = jnp.concatenate([x.astype(F32) for x in tiles], axis=0).astype(BF16)
        for c in range(8):
            states[c, ROWS * i + 8 * t:ROWS * i + 8 * t + 16] = rows[:, 128 * c:128 * (c + 1)]

    loads[1].wait()
    for i in range(2):
        for t in (2, 4, 6):
            put_state(i, t)
    for load in loads[2:4] + loads[5:]:
        load.wait()
    bands = [rband[i] for i in range(2)]

    def put_windows(at, ext):
        for k, block in enumerate(windows(*ext, TILES)):
            win[at + k] = block.astype(BF16)

    def with_edges(r, w, x):
        return jnp.concatenate(
            [
                w[0:4], r[72:76], w[4:8], r[4:8], w[8:12], r[12:16],
                r[16:64],
                r[64:68], x[0:4], r[72:76], x[4:8], r[4:8], x[8:12],
            ],
            axis=0,
        )

    def without_edges(r):
        return jnp.concatenate([r[72:76], r[72:76], r, r[4:8], r[4:8]], axis=0)

    for step in range(STEPS):
        if step == 0:
            for d in (2, 3):
                state_message(d).wait_recv()
            for i in range(2):
                for t in (0, 8):
                    put_state(i, t)
        for i in range(2):
            for b in range(8):
                x = jnp.concatenate(
                    [states[cidx[bands[i], k, b], ROWS * i:ROWS * (i + 1)] for k in range(2)], axis=1
                )
                w = jnp.concatenate(
                    [coup[bands[i], (2 * b + k) * 128:(2 * b + k + 1) * 128] for k in range(2)], axis=1
                )
                pre[i, b] = dot_nt(x, w)
        if step == 0:
            wait_recv(step, (3, 5, 7))
            pl.when(is_first)(send_west)
            wait_recv(step, (2,))
        for p in range(4):
            ext = []
            for k in range(3):
                r = raw[step, p, k].astype(F32)
                if step == 0:
                    w, x = (edge_in[side, p, k].astype(F32) for side in range(2))
                    ext.append(with_edges(r, w, x))
                else:
                    ext.append(without_edges(r))
            put_windows(5 + 5 * p, ext)

        wait_recv(step, (0, 1) + ((4, 6) if step == 0 else ()))
        for side, p in enumerate((3, 0)):
            ext = []
            for k in range(3):
                r = halo[step, side, k].astype(F32)
                if step == 0:
                    w, x = (edge_in[2 + s, p, k].astype(F32) for s in range(2))
                    ext.append(with_edges(r, w, x))
                else:
                    ext.append(without_edges(r))
            put_windows(25 * side, ext)

        for i in range(2):
            for b in range(8):
                x = win[10 * i + qidx[bands[i], b]]
                w = drive[bands[i], 128 * b:128 * (b + 1)]
                new = jnp.tanh(pre[i, b] + dot_nt(x, w))
                states[b, ROWS * i:ROWS * (i + 1)] = new.astype(BF16)
                if step == STEPS - 1:
                    for j in range(16):
                        at = row_of(j, 0)
                        state_out[i, j, :, 128 * b:128 * (b + 1)] = new[at:at + 4].astype(BF16)
        if step == 0:
            loads[4].wait()
        x = jnp.concatenate([states[c] for c in range(8)], axis=1)
        if step < STEPS - 1:
            for h in range(2):
                y = dot_nt(x, read[0, 320 * h:320 * h + 320])
                y = jnp.concatenate([y, jnp.zeros((2 * ROWS, 64), F32)], axis=1)
                for i in range(2):
                    put_raw(
                        step + 1, 2 * i + h,
                        tuple(y[ROWS * i:ROWS * (i + 1), 128 * k:128 * (k + 1)] for k in range(3)),
                    )
                by_side(lambda d: message(step + 1, d).start(), (h,))
        else:
            for dy in range(4):
                y = dot_nt(x, read[0, 160 * dy:160 * dy + 160])
                for i in range(2):
                    at = ROWS * (4 * i + dy)
                    ta[at:at + ROWS] = y[ROWS * i:ROWS * (i + 1), 0:128]
                    tb[at:at + ROWS, 0:32] = y[ROWS * i:ROWS * (i + 1), 128:160]

    for m in range(4):
        cols = []
        prev = None
        for j in range(16):
            off = (160 * j) % 128
            v0 = ta[pl.ds(row_of(j, m), 8, stride=ROWS), :]
            v1 = tb[pl.ds(row_of(j, m), 8, stride=ROWS), :]
            if off == 0:
                cols.append(v0)
                prev = (v0, v1, 0)
                continue
            r0, r1 = roll(v0, off), roll(v1, off)
            p0, p1, po = prev
            cols.append(jnp.where(lane8 < po, p0, jnp.where(lane8 < po + 32, p1, r0)))
            prev = (r0, r1, off)
            if off == 96:
                cols.append(jnp.where(lane8 < 96, r0, r1))
        for k in range(20):
            field_out[m, :, 128 * k:128 * (k + 1)] = cols[k].astype(BF16)

    by_side(lambda d: message(0, d).wait_send())
    for d in (2, 3):
        state_message(d).wait_send()
    for step in range(1, STEPS):
        by_side(lambda d: message(step, d).wait_send(), (0, 1))


def deliver(field_ref, state_ref, field_out, state_out, sems):
    copies = [
        pltpu.make_async_copy(field_ref, field_out, sems.at[0]),
        pltpu.make_async_copy(state_ref, state_out, sems.at[1]),
    ]
    for copy in copies:
        copy.start()
    for copy in copies:
        copy.wait()


def per_device(field_state, reservoir_state, coupling_blocks, coupling_index, input_blocks, input_index, readout, region_band):
    hbm = pl.BlockSpec(memory_space=pltpu.HBM)
    vmem = pl.BlockSpec(memory_space=pltpu.VMEM)
    field, state = pl.pallas_call(
        kernel,
        out_shape=(
            pltpu.VMEM(field_state.shape, BF16),
            pltpu.VMEM(reservoir_state.shape, BF16),
        ),
        in_specs=[hbm] * 8,
        out_specs=(vmem, vmem),
        scratch_shapes=[
            pltpu.SMEM((2, 2, 8), jnp.int32),
            pltpu.SMEM((2, 8), jnp.int32),
            pltpu.SMEM((2,), jnp.int32),
            pltpu.VMEM(field_state.shape, BF16),
            pltpu.VMEM(reservoir_state.shape, BF16),
            pltpu.VMEM(coupling_blocks.shape, BF16),
            pltpu.VMEM(input_blocks.shape, BF16),
            pltpu.VMEM(readout.shape, BF16),
            pltpu.VMEM((8, 2 * ROWS, 128), BF16),
            pltpu.VMEM((2, 8, ROWS, 128), F32),
            pltpu.VMEM((30, ROWS, 128), BF16),
            pltpu.VMEM((STEPS, 4, 3, ROWS, 128), BF16),
            pltpu.VMEM((STEPS, 2, 3, ROWS, 128), BF16),
            pltpu.VMEM((2, 4, 3, 16, 128), BF16),
            pltpu.VMEM((4, 4, 3, 16, 128), BF16),
            pltpu.VMEM((2, 2, 2, 4, 1024), BF16),
            pltpu.VMEM((8 * ROWS, 128), F32),
            pltpu.VMEM((8 * ROWS, 128), F32),
            pltpu.SemaphoreType.DMA((8,)),
            pltpu.SemaphoreType.DMA((STEPS, 10)),
            pltpu.SemaphoreType.DMA((STEPS, 10)),
            pltpu.SemaphoreType.REGULAR,
        ],
        compiler_params=pltpu.CompilerParams(
            collective_id=0, has_side_effects=True, vmem_limit_bytes=32 * 1024 * 1024
        ),
        name="forecast",
    )(
        *(
            pltpu.with_memory_space_constraint(x, pltpu.HBM)
            for x in (
                jnp.swapaxes(coupling_index, 1, 2), input_index, region_band,
                field_state, reservoir_state, coupling_blocks, input_blocks, readout,
            )
        )
    )
    return pl.pallas_call(
        deliver,
        out_shape=(
            jax.ShapeDtypeStruct(field_state.shape, BF16),
            jax.ShapeDtypeStruct(reservoir_state.shape, BF16),
        ),
        in_specs=[vmem] * 2,
        out_specs=(hbm, hbm),
        scratch_shapes=[pltpu.SemaphoreType.DMA((2,))],
        compiler_params=pltpu.CompilerParams(vmem_limit_bytes=32 * 1024 * 1024),
        name="deliver",
    )(*(pltpu.with_memory_space_constraint(x, pltpu.VMEM) for x in (field, state)))


def solution(mesh):
    return jax.shard_map(
        per_device,
        mesh=mesh,
        in_specs=(
            P(None, "lat", "lon"),
            P("lat", "lon", None, None),
            P("lat", None, None),
            P("lat", None, None),
            P("lat", None, None),
            P("lat", None),
            P("lat", None, None),
            P("lat"),
        ),
        out_specs=(P(None, "lat", "lon"), P("lat", "lon", None, None)),
        check_vma=False,
    )
```

```python
import functools

import jax
import jax.numpy as jnp
from jax import lax
from jax.experimental import pallas as pl
from jax.experimental.pallas import tpu as pltpu
from jax.sharding import PartitionSpec as P

MESH = pl.DeviceIdType.MESH
STEPS = 3
F32 = jnp.float32
BF16 = jnp.bfloat16
TILES = 10
ROWS = 8 * TILES

DIRS = ((-1, 0), (1, 0), (0, -1), (0, 1), (-1, -1), (-1, 1), (1, -1), (1, 1))


def dot_nt(x, w):
    return lax.dot_general(x, w, (((1,), (1,)), ((), ())), preferred_element_type=F32)


def row_of(column, member):
    at = column + 2
    return at % TILES * 8 + at // TILES * 4 + member


def lanes(rows):
    return lax.broadcasted_iota(jnp.int32, (rows, 128), 1)


def roll(x, by):
    return pltpu.roll(x, by, 1)


def minus_parts(r0, r1, r2):
    lane = lanes(r0.shape[0])
    b0 = jnp.where(lane < 48, roll(r0, 48), roll(r1, 48))
    r2r = roll(r2, 80)
    b2 = jnp.where(lane < 80, roll(r1, 80), r2r)
    return b0, b2, r2r


def plus_parts(r0, r1):
    r0r = roll(r0, 112)
    return r0r, r0r, roll(r1, 16)


def windows(r0, r1, r2, n):
    rows = 8 * n
    lane = lanes(rows)
    m = slice(0, rows)
    c = slice(8, rows + 8)
    p = slice(16, rows + 16)
    m0, m2, m3 = minus_parts(r0[m], r1[m], r2[m])
    p1, p2, p4 = plus_parts(r0[p], r1[p])
    c0 = roll(r0[c], 80)
    c1 = roll(r1[c], 80)
    d1 = roll(r1[c], 112)
    d2 = roll(r2[c], 112)
    b0 = jnp.where(lane < 80, m0, c0)
    b1 = jnp.where(lane < 80, c0, jnp.where(lane < 112, c1, p1))
    b2 = jnp.where(lane < 64, p2, m2)
    b3 = jnp.where(lane < 16, m3, jnp.where(lane < 112, d1, d2))
    b4 = jnp.where(lane < 48, d2, p4)
    return b0, b1, b2, b3, b4


def kernel(
    cidx_hbm, qidx_hbm, rband_hbm,
    field_hbm, state_hbm, coup_hbm, drive_hbm, read_hbm,
    field_out, state_out,
    cidx, qidx, rband,
    field_in, state_in, coup, drive, read,
    states, pre, win, raw, halo, edge, edge_in, state_edge, ta, tb, ea, eb,
    local_sem, send_sem, recv_sem, ready,
):
    lat, lon = lax.axis_index("lat"), lax.axis_index("lon")
    nlat, nlon = lax.axis_size("lat"), lax.axis_size("lon")
    west, east = lax.rem(lon + nlon - 1, nlon), lax.rem(lon + 1, nlon)
    has_south = lat > 0
    has_north = lat < nlat - 1

    def target(d):
        dl, do = DIRS[d]
        return (lat + dl, west if do < 0 else (east if do > 0 else lon))

    def by_side(fn, dirs=range(8)):
        for d in dirs:
            dl = DIRS[d][0]
            if dl == 0:
                fn(d)
            else:
                pl.when(has_south if dl < 0 else has_north)(functools.partial(fn, d))

    is_first = lon == 0
    is_last = lon == nlon - 1
    is_before_last = lon == nlon - 2
    greeted = 1 + has_south.astype(jnp.int32) + has_north.astype(jnp.int32)

    barrier = pltpu.get_barrier_semaphore()

    def greet(d):
        pl.semaphore_signal(barrier, inc=1, device_id=target(d), device_id_type=MESH)

    by_side(greet, (4, 6, 2))

    @pl.when(jnp.logical_not(is_last))
    def _():
        by_side(greet, (0, 1))
        pl.when(jnp.logical_not(is_before_last))(lambda: by_side(greet, (5, 7, 3)))

    loads = [
        pltpu.make_async_copy(src, dst, local_sem.at[n])
        for n, (src, dst) in enumerate(
            ((field_hbm.at[:, :, 2048:2560], field_in.at[:, :, 2048:2560]),
             (field_hbm.at[:, :, 0:2048], field_in.at[:, :, 0:2048]),
             (state_hbm, state_in), (coup_hbm, coup), (drive_hbm, drive), (read_hbm, read),
             (cidx_hbm, cidx), (qidx_hbm, qidx), (rband_hbm, rband))
        )
    ]
    for load in loads:
        load.start()

    def remote(src, dst, step, n, d):
        return pltpu.make_async_remote_copy(
            src_ref=src, dst_ref=dst, send_sem=send_sem.at[step, n], recv_sem=recv_sem.at[step, n],
            device_id=target(d), device_id_type=MESH,
        )

    def message(step, d):
        if d == 0:
            return remote(raw.at[step, 0], halo.at[step, 1], step, d, d)
        if d == 1:
            return remote(raw.at[step, 3], halo.at[step, 0], step, d, d)
        dl, do = DIRS[d]
        side, into = (0, 1) if do < 0 else (1, 0)
        if dl == 0:
            return remote(edge.at[side], edge_in.at[into], step, d, d)
        pair = 0 if dl < 0 else 3
        return remote(edge.at[side, pair], edge_in.at[2 + into, pair], step, d, d)

    def state_message(d):
        side, into = (0, 1) if DIRS[d][1] < 0 else (1, 0)
        return remote(state_hbm.at[:, pl.ds(14 * side, 2)], state_edge.at[into], 0, 6 + d, d)

    def wait_recv(step, dirs):
        for d in dirs:
            dl = DIRS[d][0]
            if dl == 0:
                message(step, d).wait_recv()
            else:
                pl.when(has_north if dl < 0 else has_south)(message(step, d).wait_recv)

    def put_raw(step, pair, r):
        for k in range(3):
            raw[step, pair, k] = r[k].astype(BF16)

    @pl.when(is_last)
    def _():
        pl.semaphore_wait(barrier, greeted)
        state_message(3).start()

    lane8 = lanes(8)

    def to_regions(columns, row, stride, to_a, to_b):
        for m in range(4):
            f = {}
            for j in columns:
                q, off = (160 * j) // 128, (160 * j) % 128
                for k in (q, q + 1):
                    if k not in f:
                        f[k] = field_in[m, :, 128 * k:128 * (k + 1)].astype(F32)
                if off == 0:
                    w0, w1 = f[q], f[q + 1]
                else:
                    w1 = roll(f[q + 1], 128 - off)
                    w0 = jnp.where(lane8 < 128 - off, roll(f[q], 128 - off), w1)
                to_a[pl.ds(row(j, m), 8, stride=stride), :] = w0
                to_b[pl.ds(row(j, m), 8, stride=stride), :] = w1

    def to_pair(p, rows, from_a, from_b):
        lane = lanes(rows)
        lo, mid, hi = 2 * p * rows, (2 * p + 1) * rows, (2 * p + 2) * rows
        a0, a1 = from_a[lo:mid], from_b[lo:mid]
        b0, b1 = roll(from_a[mid:hi], 32), roll(from_b[mid:hi], 32)
        return a0, jnp.where(lane < 32, a1, b0), jnp.where(lane < 32, b0, b1)

    def put_edge(side, first):
        to_regions(range(first, first + 3), lambda j, m: 4 * (j - first) + m, 16, ea.at[side], eb.at[side])
        for p in range(4):
            for k, rows in enumerate(to_pair(p, 16, ea.at[side], eb.at[side])):
                edge[side, p, k] = rows.astype(BF16)

    def start(d):
        message(0, d).start()

    loads[0].wait()
    put_edge(1, 13)
    pl.when(is_last)(lambda: by_side(start, (5, 7, 3)))
    loads[1].wait()
    put_edge(0, 0)
    to_regions(range(16), row_of, ROWS, ta, tb)
    for p in range(4):
        put_raw(0, p, to_pair(p, ROWS, ta, tb))

    @pl.when(lat == 0)
    def _():
        halo[:, 0] = jnp.zeros(halo.shape[:1] + halo.shape[2:], BF16)
        edge_in[2:4, 3] = jnp.zeros((2,) + edge_in.shape[2:], BF16)

    @pl.when(lat == nlat - 1)
    def _():
        halo[:, 1] = jnp.zeros(halo.shape[:1] + halo.shape[2:], BF16)
        edge_in[2:4, 0] = jnp.zeros((2,) + edge_in.shape[2:], BF16)

    def send_west():
        by_side(start, (4, 6, 2))
        state_message(2).start()

    @pl.when(is_last)
    def _():
        pl.semaphore_wait(ready, 1)
        by_side(start, (0, 1))
        send_west()

    @pl.when(jnp.logical_not(is_last))
    def _():
        pl.semaphore_wait(barrier, 2 * greeted - 1 + jnp.where(is_first, 0, greeted))

        @pl.when(is_before_last)
        def _():
            pl.semaphore_signal(ready, inc=1, device_id=(lat, east), device_id_type=MESH)

        by_side(start, (5, 7, 3))
        state_message(3).start()
        by_side(start, (0, 1))
        pl.when(jnp.logical_not(is_first))(send_west)

    def put_state(i, t):
        tiles = []
        for s in (t, t + 1):
            tiles.append(state_in[i, s - 2] if s >= 2 else state_edge[0, i, s])
            tiles.append(state_in[i, s + 8] if s < 8 else state_edge[1, i, s - 8])
        rows = jnp.concatenate([x.astype(F32) for x in tiles], axis=0).astype(BF16)
        for c in range(8):
            states[c, ROWS * i + 8 * t:ROWS * i + 8 * t + 16] = rows[:, 128 * c:128 * (c + 1)]

    loads[2].wait()
    for i in range(2):
        for t in (2, 4, 6):
            put_state(i, t)
    for load in loads[3:5] + loads[6:]:
        load.wait()
    bands = [rband[i] for i in range(2)]

    def put_windows(at, ext):
        for k, block in enumerate(windows(*ext, TILES)):
            win[at + k] = block.astype(BF16)

    def with_edges(r, w, x):
        return jnp.concatenate(
            [
                w[0:4], r[72:76], w[4:8], r[4:8], w[8:12], r[12:16],
                r[16:64],
                r[64:68], x[0:4], r[72:76], x[4:8], r[4:8], x[8:12],
            ],
            axis=0,
        )

    def without_edges(r):
        return jnp.concatenate([r[72:76], r[72:76], r, r[4:8], r[4:8]], axis=0)

    for step in range(STEPS):
        if step == 0:
            for d in (2, 3):
                state_message(d).wait_recv()
            for i in range(2):
                for t in (0, 8):
                    put_state(i, t)
        for i in range(2):
            for b in range(8):
                x = jnp.concatenate(
                    [states[cidx[bands[i], k, b], ROWS * i:ROWS * (i + 1)] for k in range(2)], axis=1
                )
                w = jnp.concatenate(
                    [coup[bands[i], (2 * b + k) * 128:(2 * b + k + 1) * 128] for k in range(2)], axis=1
                )
                pre[i, b] = dot_nt(x, w)
        if step == 0:
            wait_recv(step, (3, 5, 7))
            pl.when(is_first)(send_west)
            wait_recv(step, (2,))
        for p in range(4):
            ext = []
            for k in range(3):
                r = raw[step, p, k].astype(F32)
                if step == 0:
                    w, x = (edge_in[side, p, k].astype(F32) for side in range(2))
                    ext.append(with_edges(r, w, x))
                else:
                    ext.append(without_edges(r))
            put_windows(5 + 5 * p, ext)

        wait_recv(step, (0, 1) + ((4, 6) if step == 0 else ()))
        for side, p in enumerate((3, 0)):
            ext = []
            for k in range(3):
                r = halo[step, side, k].astype(F32)
                if step == 0:
                    w, x = (edge_in[2 + s, p, k].astype(F32) for s in range(2))
                    ext.append(with_edges(r, w, x))
                else:
                    ext.append(without_edges(r))
            put_windows(25 * side, ext)

        for i in range(2):
            for b in range(8):
                x = win[10 * i + qidx[bands[i], b]]
                w = drive[bands[i], 128 * b:128 * (b + 1)]
                new = jnp.tanh(pre[i, b] + dot_nt(x, w))
                states[b, ROWS * i:ROWS * (i + 1)] = new.astype(BF16)
                if step == STEPS - 1:
                    for j in range(16):
                        at = row_of(j, 0)
                        state_out[i, j, :, 128 * b:128 * (b + 1)] = new[at:at + 4].astype(BF16)
        if step == 0:
            loads[5].wait()
        x = jnp.concatenate([states[c] for c in range(8)], axis=1)
        if step < STEPS - 1:
            first = jnp.where(lat < nlat // 2, 1, 0)
            for n in range(2):
                h = first if n == 0 else 1 - first
                y = dot_nt(x, read[0, pl.ds(pl.multiple_of(320 * h, 320), 320)])
                y = jnp.concatenate([y, jnp.zeros((2 * ROWS, 64), F32)], axis=1)
                for i in range(2):
                    put_raw(
                        step + 1, 2 * i + h,
                        tuple(y[ROWS * i:ROWS * (i + 1), 128 * k:128 * (k + 1)] for k in range(3)),
                    )
                pl.when((h == 0) & has_south)(message(step + 1, 0).start)
                pl.when((h == 1) & has_north)(message(step + 1, 1).start)
        else:
            for dy in range(4):
                y = dot_nt(x, read[0, 160 * dy:160 * dy + 160])
                for i in range(2):
                    at = ROWS * (4 * i + dy)
                    ta[at:at + ROWS] = y[ROWS * i:ROWS * (i + 1), 0:128]
                    tb[at:at + ROWS, 0:32] = y[ROWS * i:ROWS * (i + 1), 128:160]

    for m in range(4):
        cols = []
        prev = None
        for j in range(16):
            off = (160 * j) % 128
            v0 = ta[pl.ds(row_of(j, m), 8, stride=ROWS), :]
            v1 = tb[pl.ds(row_of(j, m), 8, stride=ROWS), :]
            if off == 0:
                cols.append(v0)
                prev = (v0, v1, 0)
                continue
            r0, r1 = roll(v0, off), roll(v1, off)
            p0, p1, po = prev
            cols.append(jnp.where(lane8 < po, p0, jnp.where(lane8 < po + 32, p1, r0)))
            prev = (r0, r1, off)
            if off == 96:
                cols.append(jnp.where(lane8 < 96, r0, r1))
        for k in range(20):
            field_out[m, :, 128 * k:128 * (k + 1)] = cols[k].astype(BF16)

    by_side(lambda d: message(0, d).wait_send())
    for d in (2, 3):
        state_message(d).wait_send()
    for step in range(1, STEPS):
        by_side(lambda d: message(step, d).wait_send(), (0, 1))


def deliver(field_ref, state_ref, field_out, state_out, sems):
    copies = [
        pltpu.make_async_copy(field_ref, field_out, sems.at[0]),
        pltpu.make_async_copy(state_ref, state_out, sems.at[1]),
    ]
    for copy in copies:
        copy.start()
    for copy in copies:
        copy.wait()


def per_device(field_state, reservoir_state, coupling_blocks, coupling_index, input_blocks, input_index, readout, region_band):
    hbm = pl.BlockSpec(memory_space=pltpu.HBM)
    vmem = pl.BlockSpec(memory_space=pltpu.VMEM)
    field, state = pl.pallas_call(
        kernel,
        out_shape=(
            pltpu.VMEM(field_state.shape, BF16),
            pltpu.VMEM(reservoir_state.shape, BF16),
        ),
        in_specs=[hbm] * 8,
        out_specs=(vmem, vmem),
        scratch_shapes=[
            pltpu.SMEM((2, 2, 8), jnp.int32),
            pltpu.SMEM((2, 8), jnp.int32),
            pltpu.SMEM((2,), jnp.int32),
            pltpu.VMEM(field_state.shape, BF16),
            pltpu.VMEM(reservoir_state.shape, BF16),
            pltpu.VMEM(coupling_blocks.shape, BF16),
            pltpu.VMEM(input_blocks.shape, BF16),
            pltpu.VMEM(readout.shape, BF16),
            pltpu.VMEM((8, 2 * ROWS, 128), BF16),
            pltpu.VMEM((2, 8, ROWS, 128), F32),
            pltpu.VMEM((30, ROWS, 128), BF16),
            pltpu.VMEM((STEPS, 4, 3, ROWS, 128), BF16),
            pltpu.VMEM((STEPS, 2, 3, ROWS, 128), BF16),
            pltpu.VMEM((2, 4, 3, 16, 128), BF16),
            pltpu.VMEM((4, 4, 3, 16, 128), BF16),
            pltpu.VMEM((2, 2, 2, 4, 1024), BF16),
            pltpu.VMEM((8 * ROWS, 128), F32),
            pltpu.VMEM((8 * ROWS, 128), F32),
            pltpu.VMEM((2, 128, 128), F32),
            pltpu.VMEM((2, 128, 128), F32),
            pltpu.SemaphoreType.DMA((9,)),
            pltpu.SemaphoreType.DMA((STEPS, 10)),
            pltpu.SemaphoreType.DMA((STEPS, 10)),
            pltpu.SemaphoreType.REGULAR,
        ],
        compiler_params=pltpu.CompilerParams(
            collective_id=0, has_side_effects=True, vmem_limit_bytes=32 * 1024 * 1024
        ),
        name="forecast",
    )(
        *(
            pltpu.with_memory_space_constraint(x, pltpu.HBM)
            for x in (
                jnp.swapaxes(coupling_index, 1, 2), input_index, region_band,
                field_state, reservoir_state, coupling_blocks, input_blocks, readout,
            )
        )
    )
    return pl.pallas_call(
        deliver,
        out_shape=(
            jax.ShapeDtypeStruct(field_state.shape, BF16),
            jax.ShapeDtypeStruct(reservoir_state.shape, BF16),
        ),
        in_specs=[vmem] * 2,
        out_specs=(hbm, hbm),
        scratch_shapes=[pltpu.SemaphoreType.DMA((2,))],
        compiler_params=pltpu.CompilerParams(vmem_limit_bytes=32 * 1024 * 1024),
        name="deliver",
    )(*(pltpu.with_memory_space_constraint(x, pltpu.VMEM) for x in (field, state)))


def solution(mesh):
    return jax.shard_map(
        per_device,
        mesh=mesh,
        in_specs=(
            P(None, "lat", "lon"),
            P("lat", "lon", None, None),
            P("lat", None, None),
            P("lat", None, None),
            P("lat", None, None),
            P("lat", None),
            P("lat", None, None),
            P("lat"),
        ),
        out_specs=(P(None, "lat", "lon"), P("lat", "lon", None, None)),
        check_vma=False,
    )
```

```python
import functools

import jax
import jax.numpy as jnp
from jax import lax
from jax.experimental import pallas as pl
from jax.experimental.pallas import tpu as pltpu
from jax.sharding import PartitionSpec as P

MESH = pl.DeviceIdType.MESH
STEPS = 3
F32 = jnp.float32
BF16 = jnp.bfloat16
TILES = 10
ROWS = 8 * TILES

DIRS = ((-1, 0), (1, 0), (0, -1), (0, 1), (-1, -1), (-1, 1), (1, -1), (1, 1))


def dot_nt(x, w):
    return lax.dot_general(x, w, (((1,), (1,)), ((), ())), preferred_element_type=F32)


def row_of(column, member):
    at = column + 2
    return at % TILES * 8 + at // TILES * 4 + member


def lanes(rows):
    return lax.broadcasted_iota(jnp.int32, (rows, 128), 1)


def roll(x, by):
    return pltpu.roll(x, by, 1)


def minus_parts(r0, r1, r2):
    lane = lanes(r0.shape[0])
    b0 = jnp.where(lane < 48, roll(r0, 48), roll(r1, 48))
    r2r = roll(r2, 80)
    b2 = jnp.where(lane < 80, roll(r1, 80), r2r)
    return b0, b2, r2r


def plus_parts(r0, r1):
    r0r = roll(r0, 112)
    return r0r, r0r, roll(r1, 16)


def windows(r0, r1, r2, n):
    rows = 8 * n
    lane = lanes(rows)
    m = slice(0, rows)
    c = slice(8, rows + 8)
    p = slice(16, rows + 16)
    m0, m2, m3 = minus_parts(r0[m], r1[m], r2[m])
    p1, p2, p4 = plus_parts(r0[p], r1[p])
    c0 = roll(r0[c], 80)
    c1 = roll(r1[c], 80)
    d1 = roll(r1[c], 112)
    d2 = roll(r2[c], 112)
    b0 = jnp.where(lane < 80, m0, c0)
    b1 = jnp.where(lane < 80, c0, jnp.where(lane < 112, c1, p1))
    b2 = jnp.where(lane < 64, p2, m2)
    b3 = jnp.where(lane < 16, m3, jnp.where(lane < 112, d1, d2))
    b4 = jnp.where(lane < 48, d2, p4)
    return b0, b1, b2, b3, b4


def kernel(
    cidx_hbm, qidx_hbm, rband_hbm,
    field_hbm, state_hbm, coup_hbm, drive_hbm, read_hbm,
    field_out, state_out,
    cidx, qidx, rband,
    field_in, state_in, coup, drive, read,
    states, pre, win, raw, halo, edge, edge_in, state_edge, ta, tb, ea, eb,
    local_sem, send_sem, recv_sem, ready,
):
    lat, lon = lax.axis_index("lat"), lax.axis_index("lon")
    nlat, nlon = lax.axis_size("lat"), lax.axis_size("lon")
    west, east = lax.rem(lon + nlon - 1, nlon), lax.rem(lon + 1, nlon)
    has_south = lat > 0
    has_north = lat < nlat - 1

    def target(d):
        dl, do = DIRS[d]
        return (lat + dl, west if do < 0 else (east if do > 0 else lon))

    def by_side(fn, dirs=range(8)):
        for d in dirs:
            dl = DIRS[d][0]
            if dl == 0:
                fn(d)
            else:
                pl.when(has_south if dl < 0 else has_north)(functools.partial(fn, d))

    loads = [
        pltpu.make_async_copy(src, dst, local_sem.at[n])
        for n, (src, dst) in enumerate(
            ((field_hbm.at[:, :, 2048:2560], field_in.at[:, :, 2048:2560]),
             (field_hbm.at[:, :, 0:2048], field_in.at[:, :, 0:2048]),
             (state_hbm, state_in), (coup_hbm, coup), (drive_hbm, drive), (read_hbm, read),
             (cidx_hbm, cidx), (qidx_hbm, qidx), (rband_hbm, rband))
        )
    ]
    loads[0].start()

    is_first = lon == 0
    is_last = lon == nlon - 1
    is_before_last = lon == nlon - 2
    greeted = 1 + has_south.astype(jnp.int32) + has_north.astype(jnp.int32)

    barrier = pltpu.get_barrier_semaphore()

    def greet(d):
        pl.semaphore_signal(barrier, inc=1, device_id=target(d), device_id_type=MESH)

    by_side(greet, (4, 6, 2))

    @pl.when(jnp.logical_not(is_last))
    def _():
        by_side(greet, (0, 1))
        pl.when(jnp.logical_not(is_before_last))(lambda: by_side(greet, (5, 7, 3)))

    for load in loads[1:]:
        load.start()

    def remote(src, dst, step, n, d):
        return pltpu.make_async_remote_copy(
            src_ref=src, dst_ref=dst, send_sem=send_sem.at[step, n], recv_sem=recv_sem.at[step, n],
            device_id=target(d), device_id_type=MESH,
        )

    def message(step, d):
        if d == 0:
            return remote(raw.at[step, 0], halo.at[step, 1], step, d, d)
        if d == 1:
            return remote(raw.at[step, 3], halo.at[step, 0], step, d, d)
        dl, do = DIRS[d]
        side, into = (0, 1) if do < 0 else (1, 0)
        if dl == 0:
            return remote(edge.at[side], edge_in.at[into], step, d, d)
        pair = 0 if dl < 0 else 3
        return remote(edge.at[side, pair], edge_in.at[2 + into, pair], step, d, d)

    def state_message(d):
        side, into = (0, 1) if DIRS[d][1] < 0 else (1, 0)
        return remote(state_hbm.at[:, pl.ds(14 * side, 2)], state_edge.at[into], 0, 6 + d, d)

    def wait_recv(step, dirs):
        for d in dirs:
            dl = DIRS[d][0]
            if dl == 0:
                message(step, d).wait_recv()
            else:
                pl.when(has_north if dl < 0 else has_south)(message(step, d).wait_recv)

    def put_raw(step, pair, r):
        for k in range(3):
            raw[step, pair, k] = r[k].astype(BF16)

    @pl.when(is_last)
    def _():
        pl.semaphore_wait(barrier, greeted)
        state_message(3).start()

    lane8 = lanes(8)

    def to_regions(columns, row, stride, to_a, to_b):
        for m in range(4):
            f = {}
            for j in columns:
                q, off = (160 * j) // 128, (160 * j) % 128
                for k in (q, q + 1):
                    if k not in f:
                        f[k] = field_in[m, :, 128 * k:128 * (k + 1)].astype(F32)
                if off == 0:
                    w0, w1 = f[q], f[q + 1]
                else:
                    w1 = roll(f[q + 1], 128 - off)
                    w0 = jnp.where(lane8 < 128 - off, roll(f[q], 128 - off), w1)
                to_a[pl.ds(row(j, m), 8, stride=stride), :] = w0
                to_b[pl.ds(row(j, m), 8, stride=stride), :] = w1

    def to_pair(p, rows, from_a, from_b):
        lane = lanes(rows)
        lo, mid, hi = 2 * p * rows, (2 * p + 1) * rows, (2 * p + 2) * rows
        a0, a1 = from_a[lo:mid], from_b[lo:mid]
        b0, b1 = roll(from_a[mid:hi], 32), roll(from_b[mid:hi], 32)
        return a0, jnp.where(lane < 32, a1, b0), jnp.where(lane < 32, b0, b1)

    def put_edge(side, first):
        to_regions(range(first, first + 3), lambda j, m: 4 * (j - first) + m, 16, ea.at[side], eb.at[side])
        for p in range(4):
            for k, rows in enumerate(to_pair(p, 16, ea.at[side], eb.at[side])):
                edge[side, p, k] = rows.astype(BF16)

    def start(d):
        message(0, d).start()

    loads[0].wait()
    put_edge(1, 13)
    pl.when(is_last)(lambda: by_side(start, (5, 7, 3)))
    loads[1].wait()
    put_edge(0, 0)
    to_regions(range(16), row_of, ROWS, ta, tb)
    for p in range(4):
        put_raw(0, p, to_pair(p, ROWS, ta, tb))

    @pl.when(lat == 0)
    def _():
        halo[:, 0] = jnp.zeros(halo.shape[:1] + halo.shape[2:], BF16)
        edge_in[2:4, 3] = jnp.zeros((2,) + edge_in.shape[2:], BF16)

    @pl.when(lat == nlat - 1)
    def _():
        halo[:, 1] = jnp.zeros(halo.shape[:1] + halo.shape[2:], BF16)
        edge_in[2:4, 0] = jnp.zeros((2,) + edge_in.shape[2:], BF16)

    def send_west():
        by_side(start, (4, 6, 2))
        state_message(2).start()

    @pl.when(is_last)
    def _():
        pl.semaphore_wait(ready, 1)
        by_side(start, (0, 1))
        send_west()

    @pl.when(jnp.logical_not(is_last))
    def _():
        pl.semaphore_wait(barrier, 2 * greeted - 1 + jnp.where(is_first, 0, greeted))

        @pl.when(is_before_last)
        def _():
            pl.semaphore_signal(ready, inc=1, device_id=(lat, east), device_id_type=MESH)

        by_side(start, (5, 7, 3))
        state_message(3).start()
        by_side(start, (0, 1))
        pl.when(jnp.logical_not(is_first))(send_west)

    def put_state(i, t):
        tiles = []
        for s in (t, t + 1):
            tiles.append(state_in[i, s - 2] if s >= 2 else state_edge[0, i, s])
            tiles.append(state_in[i, s + 8] if s < 8 else state_edge[1, i, s - 8])
        rows = jnp.concatenate([x.astype(F32) for x in tiles], axis=0).astype(BF16)
        for c in range(8):
            states[c, ROWS * i + 8 * t:ROWS * i + 8 * t + 16] = rows[:, 128 * c:128 * (c + 1)]

    loads[2].wait()
    for i in range(2):
        for t in (2, 4, 6):
            put_state(i, t)
    for load in loads[3:5] + loads[6:]:
        load.wait()
    bands = [rband[i] for i in range(2)]

    def put_windows(at, ext):
        for k, block in enumerate(windows(*ext, TILES)):
            win[at + k] = block.astype(BF16)

    def with_edges(r, w, x):
        return jnp.concatenate(
            [
                w[0:4], r[72:76], w[4:8], r[4:8], w[8:12], r[12:16],
                r[16:64],
                r[64:68], x[0:4], r[72:76], x[4:8], r[4:8], x[8:12],
            ],
            axis=0,
        )

    def without_edges(r):
        return jnp.concatenate([r[72:76], r[72:76], r, r[4:8], r[4:8]], axis=0)

    near = jnp.where(lat < nlat // 2, 0, 1)
    for step in range(STEPS):
        if step == 0:
            for d in (2, 3):
                state_message(d).wait_recv()
            for i in range(2):
                for t in (0, 8):
                    put_state(i, t)
        for i in range(2):
            for b in range(8):
                x = jnp.concatenate(
                    [states[cidx[bands[i], k, b], ROWS * i:ROWS * (i + 1)] for k in range(2)], axis=1
                )
                w = jnp.concatenate(
                    [coup[bands[i], (2 * b + k) * 128:(2 * b + k + 1) * 128] for k in range(2)], axis=1
                )
                pre[i, b] = dot_nt(x, w)
        if step == 0:
            wait_recv(step, (3, 5, 7))
            pl.when(is_first)(send_west)
            wait_recv(step, (2,))
        for p in range(4):
            ext = []
            for k in range(3):
                r = raw[step, p, k].astype(F32)
                if step == 0:
                    w, x = (edge_in[side, p, k].astype(F32) for side in range(2))
                    ext.append(with_edges(r, w, x))
                else:
                    ext.append(without_edges(r))
            put_windows(5 + 5 * p, ext)

        def put_halo_windows(i):
            ext = []
            for k in range(3):
                r = halo[step, i, k].astype(F32)
                if step == 0:
                    w, x = (edge_in[2 + s, 3 - 3 * i, k].astype(F32) for s in range(2))
                    ext.append(with_edges(r, w, x))
                else:
                    ext.append(without_edges(r))
            for k, block in enumerate(windows(*ext, TILES)):
                win[25 * i + k] = block.astype(BF16)

        def put_new_states(i):
            band = rband[i]
            rows = pl.ds(pl.multiple_of(ROWS * i, ROWS), ROWS)
            for b in range(8):
                x = win[10 * i + qidx[band, b]]
                w = drive[band, 128 * b:128 * (b + 1)]
                new = jnp.tanh(pre[i, b] + dot_nt(x, w))
                states[b, rows] = new.astype(BF16)
                if step == STEPS - 1:
                    for j in range(16):
                        at = row_of(j, 0)
                        state_out[i, j, :, 128 * b:128 * (b + 1)] = new[at:at + 4].astype(BF16)

        if step == 0:
            wait_recv(step, (0, 1, 4, 6))
            for i in range(2):
                put_halo_windows(i)
            for i in range(2):
                put_new_states(i)
            loads[5].wait()
        else:
            for n in range(2):
                i = near if n == 0 else 1 - near
                pl.when((i == 0) & has_south)(message(step, 1).wait_recv)
                pl.when((i == 1) & has_north)(message(step, 0).wait_recv)
                put_halo_windows(i)
                put_new_states(i)
        x = jnp.concatenate([states[c] for c in range(8)], axis=1)
        if step < STEPS - 1:
            first = 1 - near
            for n in range(2):
                h = first if n == 0 else 1 - first
                y = dot_nt(x, read[0, pl.ds(pl.multiple_of(320 * h, 320), 320)])
                y = jnp.concatenate([y, jnp.zeros((2 * ROWS, 64), F32)], axis=1)
                for i in range(2):
                    put_raw(
                        step + 1, 2 * i + h,
                        tuple(y[ROWS * i:ROWS * (i + 1), 128 * k:128 * (k + 1)] for k in range(3)),
                    )
                pl.when((h == 0) & has_south)(message(step + 1, 0).start)
                pl.when((h == 1) & has_north)(message(step + 1, 1).start)
        else:
            for dy in range(4):
                y = dot_nt(x, read[0, 160 * dy:160 * dy + 160])
                for i in range(2):
                    at = ROWS * (4 * i + dy)
                    ta[at:at + ROWS] = y[ROWS * i:ROWS * (i + 1), 0:128]
                    tb[at:at + ROWS, 0:32] = y[ROWS * i:ROWS * (i + 1), 128:160]

    for m in range(4):
        cols = []
        prev = None
        for j in range(16):
            off = (160 * j) % 128
            v0 = ta[pl.ds(row_of(j, m), 8, stride=ROWS), :]
            v1 = tb[pl.ds(row_of(j, m), 8, stride=ROWS), :]
            if off == 0:
                cols.append(v0)
                prev = (v0, v1, 0)
                continue
            r0, r1 = roll(v0, off), roll(v1, off)
            p0, p1, po = prev
            cols.append(jnp.where(lane8 < po, p0, jnp.where(lane8 < po + 32, p1, r0)))
            prev = (r0, r1, off)
            if off == 96:
                cols.append(jnp.where(lane8 < 96, r0, r1))
        for k in range(20):
            field_out[m, :, 128 * k:128 * (k + 1)] = cols[k].astype(BF16)

    by_side(lambda d: message(0, d).wait_send())
    for d in (2, 3):
        state_message(d).wait_send()
    for step in range(1, STEPS):
        by_side(lambda d: message(step, d).wait_send(), (0, 1))


def deliver(field_ref, state_ref, field_out, state_out, sems):
    copies = [
        pltpu.make_async_copy(field_ref, field_out, sems.at[0]),
        pltpu.make_async_copy(state_ref, state_out, sems.at[1]),
    ]
    for copy in copies:
        copy.start()
    for copy in copies:
        copy.wait()


def per_device(field_state, reservoir_state, coupling_blocks, coupling_index, input_blocks, input_index, readout, region_band):
    hbm = pl.BlockSpec(memory_space=pltpu.HBM)
    vmem = pl.BlockSpec(memory_space=pltpu.VMEM)
    field, state = pl.pallas_call(
        kernel,
        out_shape=(
            pltpu.VMEM(field_state.shape, BF16),
            pltpu.VMEM(reservoir_state.shape, BF16),
        ),
        in_specs=[hbm] * 8,
        out_specs=(vmem, vmem),
        scratch_shapes=[
            pltpu.SMEM((2, 2, 8), jnp.int32),
            pltpu.SMEM((2, 8), jnp.int32),
            pltpu.SMEM((2,), jnp.int32),
            pltpu.VMEM(field_state.shape, BF16),
            pltpu.VMEM(reservoir_state.shape, BF16),
            pltpu.VMEM(coupling_blocks.shape, BF16),
            pltpu.VMEM(input_blocks.shape, BF16),
            pltpu.VMEM(readout.shape, BF16),
            pltpu.VMEM((8, 2 * ROWS, 128), BF16),
            pltpu.VMEM((2, 8, ROWS, 128), F32),
            pltpu.VMEM((30, ROWS, 128), BF16),
            pltpu.VMEM((STEPS, 4, 3, ROWS, 128), BF16),
            pltpu.VMEM((STEPS, 2, 3, ROWS, 128), BF16),
            pltpu.VMEM((2, 4, 3, 16, 128), BF16),
            pltpu.VMEM((4, 4, 3, 16, 128), BF16),
            pltpu.VMEM((2, 2, 2, 4, 1024), BF16),
            pltpu.VMEM((8 * ROWS, 128), F32),
            pltpu.VMEM((8 * ROWS, 128), F32),
            pltpu.VMEM((2, 128, 128), F32),
            pltpu.VMEM((2, 128, 128), F32),
            pltpu.SemaphoreType.DMA((9,)),
            pltpu.SemaphoreType.DMA((STEPS, 10)),
            pltpu.SemaphoreType.DMA((STEPS, 10)),
            pltpu.SemaphoreType.REGULAR,
        ],
        compiler_params=pltpu.CompilerParams(
            collective_id=0, has_side_effects=True, vmem_limit_bytes=32 * 1024 * 1024
        ),
        name="forecast",
    )(
        *(
            pltpu.with_memory_space_constraint(x, pltpu.HBM)
            for x in (
                jnp.swapaxes(coupling_index, 1, 2), input_index, region_band,
                field_state, reservoir_state, coupling_blocks, input_blocks, readout,
            )
        )
    )
    return pl.pallas_call(
        deliver,
        out_shape=(
            jax.ShapeDtypeStruct(field_state.shape, BF16),
            jax.ShapeDtypeStruct(reservoir_state.shape, BF16),
        ),
        in_specs=[vmem] * 2,
        out_specs=(hbm, hbm),
        scratch_shapes=[pltpu.SemaphoreType.DMA((2,))],
        compiler_params=pltpu.CompilerParams(vmem_limit_bytes=32 * 1024 * 1024),
        name="deliver",
    )(*(pltpu.with_memory_space_constraint(x, pltpu.VMEM) for x in (field, state)))


def solution(mesh):
    return jax.shard_map(
        per_device,
        mesh=mesh,
        in_specs=(
            P(None, "lat", "lon"),
            P("lat", "lon", None, None),
            P("lat", None, None),
            P("lat", None, None),
            P("lat", None, None),
            P("lat", None),
            P("lat", None, None),
            P("lat"),
        ),
        out_specs=(P(None, "lat", "lon"), P("lat", "lon", None, None)),
        check_vma=False,
    )
```

```python
import functools

import jax
import jax.numpy as jnp
from jax import lax
from jax.experimental import pallas as pl
from jax.experimental.pallas import tpu as pltpu
from jax.sharding import PartitionSpec as P

MESH = pl.DeviceIdType.MESH
STEPS = 3
F32 = jnp.float32
BF16 = jnp.bfloat16
TILES = 10
ROWS = 8 * TILES

DIRS = ((-1, 0), (1, 0), (0, -1), (0, 1), (-1, -1), (-1, 1), (1, -1), (1, 1))


def dot_nt(x, w):
    return lax.dot_general(x, w, (((1,), (1,)), ((), ())), preferred_element_type=F32)


def row_of(column, member):
    at = column + 2
    return at % TILES * 8 + at // TILES * 4 + member


def lanes(rows):
    return lax.broadcasted_iota(jnp.int32, (rows, 128), 1)


def roll(x, by):
    return pltpu.roll(x, by, 1)


def minus_parts(r0, r1, r2):
    lane = lanes(r0.shape[0])
    b0 = jnp.where(lane < 48, roll(r0, 48), roll(r1, 48))
    r2r = roll(r2, 80)
    b2 = jnp.where(lane < 80, roll(r1, 80), r2r)
    return b0, b2, r2r


def plus_parts(r0, r1):
    r0r = roll(r0, 112)
    return r0r, r0r, roll(r1, 16)


def windows(r0, r1, r2, n):
    rows = 8 * n
    lane = lanes(rows)
    m = slice(0, rows)
    c = slice(8, rows + 8)
    p = slice(16, rows + 16)
    m0, m2, m3 = minus_parts(r0[m], r1[m], r2[m])
    p1, p2, p4 = plus_parts(r0[p], r1[p])
    c0 = roll(r0[c], 80)
    c1 = roll(r1[c], 80)
    d1 = roll(r1[c], 112)
    d2 = roll(r2[c], 112)
    b0 = jnp.where(lane < 80, m0, c0)
    b1 = jnp.where(lane < 80, c0, jnp.where(lane < 112, c1, p1))
    b2 = jnp.where(lane < 64, p2, m2)
    b3 = jnp.where(lane < 16, m3, jnp.where(lane < 112, d1, d2))
    b4 = jnp.where(lane < 48, d2, p4)
    return b0, b1, b2, b3, b4


def kernel(
    cidx_hbm, qidx_hbm, rband_hbm,
    field_hbm, state_hbm, coup_hbm, drive_hbm, read_hbm,
    field_out, state_out,
    cidx, qidx, rband,
    field_in, state_in, coup, drive, read,
    states, pre, win, raw, halo, edge, edge_in, state_edge, ta, tb, ea, eb,
    local_sem, send_sem, recv_sem, ready,
):
    lat, lon = lax.axis_index("lat"), lax.axis_index("lon")
    nlat, nlon = lax.axis_size("lat"), lax.axis_size("lon")
    west, east = lax.rem(lon + nlon - 1, nlon), lax.rem(lon + 1, nlon)
    has_south = lat > 0
    has_north = lat < nlat - 1

    def target(d):
        dl, do = DIRS[d]
        return (lat + dl, west if do < 0 else (east if do > 0 else lon))

    def by_side(fn, dirs=range(8)):
        for d in dirs:
            dl = DIRS[d][0]
            if dl == 0:
                fn(d)
            else:
                pl.when(has_south if dl < 0 else has_north)(functools.partial(fn, d))

    loads = [
        pltpu.make_async_copy(src, dst, local_sem.at[n])
        for n, (src, dst) in enumerate(
            ((field_hbm.at[:, :, 2048:2560], field_in.at[:, :, 2048:2560]),
             (field_hbm.at[:, :, 0:2048], field_in.at[:, :, 0:2048]),
             (state_hbm, state_in), (coup_hbm, coup), (drive_hbm, drive), (read_hbm, read),
             (cidx_hbm, cidx), (qidx_hbm, qidx), (rband_hbm, rband))
        )
    ]
    loads[0].start()

    is_first = lon == 0
    is_last = lon == nlon - 1
    is_before_last = lon == nlon - 2
    greeted = 1 + has_south.astype(jnp.int32) + has_north.astype(jnp.int32)

    barrier = pltpu.get_barrier_semaphore()

    def greet(d):
        pl.semaphore_signal(barrier, inc=1, device_id=target(d), device_id_type=MESH)

    by_side(greet, (4, 6, 2))

    @pl.when(jnp.logical_not(is_last))
    def _():
        by_side(greet, (0, 1))
        pl.when(jnp.logical_not(is_before_last))(lambda: by_side(greet, (5, 7, 3)))

    for load in loads[1:]:
        load.start()

    def remote(src, dst, step, n, d):
        return pltpu.make_async_remote_copy(
            src_ref=src, dst_ref=dst, send_sem=send_sem.at[step, n], recv_sem=recv_sem.at[step, n],
            device_id=target(d), device_id_type=MESH,
        )

    def message(step, d):
        if d == 0:
            return remote(raw.at[step, 0], halo.at[step, 1], step, d, d)
        if d == 1:
            return remote(raw.at[step, 3], halo.at[step, 0], step, d, d)
        dl, do = DIRS[d]
        side, into = (0, 1) if do < 0 else (1, 0)
        if dl == 0:
            return remote(edge.at[side], edge_in.at[into], step, d, d)
        pair = 0 if dl < 0 else 3
        return remote(edge.at[side, pair], edge_in.at[2 + into, pair], step, d, d)

    def state_message(d):
        side, into = (0, 1) if DIRS[d][1] < 0 else (1, 0)
        return remote(state_hbm.at[:, pl.ds(14 * side, 2)], state_edge.at[into], 0, 6 + d, d)

    def wait_recv(step, dirs):
        for d in dirs:
            dl = DIRS[d][0]
            if dl == 0:
                message(step, d).wait_recv()
            else:
                pl.when(has_north if dl < 0 else has_south)(message(step, d).wait_recv)

    def put_raw(step, pair, r):
        for k in range(3):
            raw[step, pair, k] = r[k].astype(BF16)

    @pl.when(is_last)
    def _():
        pl.semaphore_wait(barrier, greeted)
        state_message(3).start()

    lane8 = lanes(8)

    def to_regions(columns, row, stride, to_a, to_b):
        for m in range(4):
            f = {}
            for j in columns:
                q, off = (160 * j) // 128, (160 * j) % 128
                for k in (q, q + 1):
                    if k not in f:
                        f[k] = field_in[m, :, 128 * k:128 * (k + 1)].astype(F32)
                if off == 0:
                    w0, w1 = f[q], f[q + 1]
                else:
                    w1 = roll(f[q + 1], 128 - off)
                    w0 = jnp.where(lane8 < 128 - off, roll(f[q], 128 - off), w1)
                to_a[pl.ds(row(j, m), 8, stride=stride), :] = w0
                to_b[pl.ds(row(j, m), 8, stride=stride), :] = w1

    def to_pair(p, rows, from_a, from_b):
        lane = lanes(rows)
        lo, mid, hi = 2 * p * rows, (2 * p + 1) * rows, (2 * p + 2) * rows
        a0, a1 = from_a[lo:mid], from_b[lo:mid]
        b0, b1 = roll(from_a[mid:hi], 32), roll(from_b[mid:hi], 32)
        return a0, jnp.where(lane < 32, a1, b0), jnp.where(lane < 32, b0, b1)

    def put_edge(side, first):
        to_regions(range(first, first + 3), lambda j, m: 4 * (j - first) + m, 16, ea.at[side], eb.at[side])
        for p in range(4):
            for k, rows in enumerate(to_pair(p, 16, ea.at[side], eb.at[side])):
                edge[side, p, k] = rows.astype(BF16)

    def start(d):
        message(0, d).start()

    loads[0].wait()
    put_edge(1, 13)
    pl.when(is_last)(lambda: by_side(start, (5, 7, 3)))
    loads[1].wait()
    put_edge(0, 0)
    to_regions(range(16), row_of, ROWS, ta, tb)
    for p in range(4):
        put_raw(0, p, to_pair(p, ROWS, ta, tb))

    @pl.when(lat == 0)
    def _():
        halo[:, 0] = jnp.zeros(halo.shape[:1] + halo.shape[2:], BF16)
        edge_in[2:4, 3] = jnp.zeros((2,) + edge_in.shape[2:], BF16)

    @pl.when(lat == nlat - 1)
    def _():
        halo[:, 1] = jnp.zeros(halo.shape[:1] + halo.shape[2:], BF16)
        edge_in[2:4, 0] = jnp.zeros((2,) + edge_in.shape[2:], BF16)

    def send_west():
        by_side(start, (4, 6, 2))
        state_message(2).start()

    @pl.when(is_last)
    def _():
        pl.semaphore_wait(ready, 1)
        by_side(start, (0, 1))
        send_west()

    @pl.when(jnp.logical_not(is_last))
    def _():
        pl.semaphore_wait(barrier, 2 * greeted - 1 + jnp.where(is_first, 0, greeted))

        @pl.when(is_before_last)
        def _():
            pl.semaphore_signal(ready, inc=1, device_id=(lat, east), device_id_type=MESH)

        by_side(start, (5, 7, 3))
        state_message(3).start()
        by_side(start, (0, 1))
        pl.when(jnp.logical_not(is_first))(send_west)

    def put_state(i, t):
        tiles = []
        for s in (t, t + 1):
            tiles.append(state_in[i, s - 2] if s >= 2 else state_edge[0, i, s])
            tiles.append(state_in[i, s + 8] if s < 8 else state_edge[1, i, s - 8])
        rows = jnp.concatenate([x.astype(F32) for x in tiles], axis=0).astype(BF16)
        for c in range(8):
            states[c, ROWS * i + 8 * t:ROWS * i + 8 * t + 16] = rows[:, 128 * c:128 * (c + 1)]

    loads[2].wait()
    for i in range(2):
        for t in (2, 4, 6):
            put_state(i, t)
    for load in loads[3:5] + loads[6:]:
        load.wait()
    bands = [rband[i] for i in range(2)]

    def put_windows(at, ext):
        for k, block in enumerate(windows(*ext, TILES)):
            win[at + k] = block.astype(BF16)

    def western(r, w):
        return jnp.concatenate(
            [w[0:4], r[72:76], w[4:8], r[4:8], w[8:12], r[12:16], r[16:40]], axis=0
        )

    def eastern(r, x):
        return jnp.concatenate(
            [r[24:64], r[64:68], x[0:4], r[72:76], x[4:8], r[4:8], x[8:12]], axis=0
        )

    starts = [(5 + 5 * p, raw.at[0, p], 0, p) for p in range(4)]
    starts += [(0, halo.at[0, 0], 2, 3), (25, halo.at[0, 1], 2, 0)]

    def put_start_windows(pairs, side, tiles, at, rows):
        for to, ref, edges, p in pairs:
            ext = [tiles(ref[k].astype(F32), edge_in[edges + side, p, k].astype(F32)) for k in range(3)]
            for k, block in enumerate(windows(*ext, rows // 8)):
                win[to + k, at:at + rows] = block.astype(BF16)

    def without_edges(r):
        return jnp.concatenate([r[72:76], r[72:76], r, r[4:8], r[4:8]], axis=0)

    near = jnp.where(lat < nlat // 2, 0, 1)
    for step in range(STEPS):
        if step == 0:
            state_message(2).wait_recv()
            for i in range(2):
                put_state(i, 8)
            wait_recv(step, (2,))
            put_start_windows(starts[:4], 1, eastern, 32, 48)
            wait_recv(step, (0, 1, 4, 6))
            put_start_windows(starts[4:], 1, eastern, 32, 48)
            state_message(3).wait_recv()
            for i in range(2):
                put_state(i, 0)
        for i in range(2):
            for b in range(8):
                x = jnp.concatenate(
                    [states[cidx[bands[i], k, b], ROWS * i:ROWS * (i + 1)] for k in range(2)], axis=1
                )
                w = jnp.concatenate(
                    [coup[bands[i], (2 * b + k) * 128:(2 * b + k + 1) * 128] for k in range(2)], axis=1
                )
                pre[i, b] = dot_nt(x, w)
        if step == 0:
            wait_recv(step, (3, 5, 7))
            put_start_windows(starts, 0, western, 0, 32)
        else:
            for p in range(4):
                put_windows(5 + 5 * p, [without_edges(raw[step, p, k].astype(F32)) for k in range(3)])

        def put_halo_windows(i):
            put_windows(25 * i, [without_edges(halo[step, i, k].astype(F32)) for k in range(3)])

        def put_new_states(i):
            band = rband[i]
            rows = pl.ds(pl.multiple_of(ROWS * i, ROWS), ROWS)
            for b in range(8):
                x = win[10 * i + qidx[band, b]]
                w = drive[band, 128 * b:128 * (b + 1)]
                new = jnp.tanh(pre[i, b] + dot_nt(x, w))
                states[b, rows] = new.astype(BF16)
                if step == STEPS - 1:
                    for j in range(16):
                        at = row_of(j, 0)
                        state_out[i, j, :, 128 * b:128 * (b + 1)] = new[at:at + 4].astype(BF16)

        if step == 0:
            for i in range(2):
                put_new_states(i)
            loads[5].wait()
        else:
            for n in range(2):
                i = near if n == 0 else 1 - near
                pl.when((i == 0) & has_south)(message(step, 1).wait_recv)
                pl.when((i == 1) & has_north)(message(step, 0).wait_recv)
                put_halo_windows(i)
                put_new_states(i)
        x = jnp.concatenate([states[c] for c in range(8)], axis=1)
        if step < STEPS - 1:
            first = 1 - near
            for n in range(2):
                h = first if n == 0 else 1 - first
                y = dot_nt(x, read[0, pl.ds(pl.multiple_of(320 * h, 320), 320)])
                y = jnp.concatenate([y, jnp.zeros((2 * ROWS, 64), F32)], axis=1)
                for i in range(2):
                    put_raw(
                        step + 1, 2 * i + h,
                        tuple(y[ROWS * i:ROWS * (i + 1), 128 * k:128 * (k + 1)] for k in range(3)),
                    )
                pl.when((h == 0) & has_south)(message(step + 1, 0).start)
                pl.when((h == 1) & has_north)(message(step + 1, 1).start)
            if step == 0:
                pl.when(is_first)(send_west)
        else:
            for dy in range(4):
                y = dot_nt(x, read[0, 160 * dy:160 * dy + 160])
                for i in range(2):
                    at = ROWS * (4 * i + dy)
                    ta[at:at + ROWS] = y[ROWS * i:ROWS * (i + 1), 0:128]
                    tb[at:at + ROWS, 0:32] = y[ROWS * i:ROWS * (i + 1), 128:160]

    for m in range(4):
        cols = []
        prev = None
        for j in range(16):
            off = (160 * j) % 128
            v0 = ta[pl.ds(row_of(j, m), 8, stride=ROWS), :]
            v1 = tb[pl.ds(row_of(j, m), 8, stride=ROWS), :]
            if off == 0:
                cols.append(v0)
                prev = (v0, v1, 0)
                continue
            r0, r1 = roll(v0, off), roll(v1, off)
            p0, p1, po = prev
            cols.append(jnp.where(lane8 < po, p0, jnp.where(lane8 < po + 32, p1, r0)))
            prev = (r0, r1, off)
            if off == 96:
                cols.append(jnp.where(lane8 < 96, r0, r1))
        for k in range(20):
            field_out[m, :, 128 * k:128 * (k + 1)] = cols[k].astype(BF16)

    by_side(lambda d: message(0, d).wait_send())
    for d in (2, 3):
        state_message(d).wait_send()
    for step in range(1, STEPS):
        by_side(lambda d: message(step, d).wait_send(), (0, 1))


def deliver(field_ref, state_ref, field_out, state_out, sems):
    copies = [
        pltpu.make_async_copy(field_ref, field_out, sems.at[0]),
        pltpu.make_async_copy(state_ref, state_out, sems.at[1]),
    ]
    for copy in copies:
        copy.start()
    for copy in copies:
        copy.wait()


def per_device(field_state, reservoir_state, coupling_blocks, coupling_index, input_blocks, input_index, readout, region_band):
    hbm = pl.BlockSpec(memory_space=pltpu.HBM)
    vmem = pl.BlockSpec(memory_space=pltpu.VMEM)
    field, state = pl.pallas_call(
        kernel,
        out_shape=(
            pltpu.VMEM(field_state.shape, BF16),
            pltpu.VMEM(reservoir_state.shape, BF16),
        ),
        in_specs=[hbm] * 8,
        out_specs=(vmem, vmem),
        scratch_shapes=[
            pltpu.SMEM((2, 2, 8), jnp.int32),
            pltpu.SMEM((2, 8), jnp.int32),
            pltpu.SMEM((2,), jnp.int32),
            pltpu.VMEM(field_state.shape, BF16),
            pltpu.VMEM(reservoir_state.shape, BF16),
            pltpu.VMEM(coupling_blocks.shape, BF16),
            pltpu.VMEM(input_blocks.shape, BF16),
            pltpu.VMEM(readout.shape, BF16),
            pltpu.VMEM((8, 2 * ROWS, 128), BF16),
            pltpu.VMEM((2, 8, ROWS, 128), F32),
            pltpu.VMEM((30, ROWS, 128), BF16),
            pltpu.VMEM((STEPS, 4, 3, ROWS, 128), BF16),
            pltpu.VMEM((STEPS, 2, 3, ROWS, 128), BF16),
            pltpu.VMEM((2, 4, 3, 16, 128), BF16),
            pltpu.VMEM((4, 4, 3, 16, 128), BF16),
            pltpu.VMEM((2, 2, 2, 4, 1024), BF16),
            pltpu.VMEM((8 * ROWS, 128), F32),
            pltpu.VMEM((8 * ROWS, 128), F32),
            pltpu.VMEM((2, 128, 128), F32),
            pltpu.VMEM((2, 128, 128), F32),
            pltpu.SemaphoreType.DMA((9,)),
            pltpu.SemaphoreType.DMA((STEPS, 10)),
            pltpu.SemaphoreType.DMA((STEPS, 10)),
            pltpu.SemaphoreType.REGULAR,
        ],
        compiler_params=pltpu.CompilerParams(
            collective_id=0, has_side_effects=True, vmem_limit_bytes=32 * 1024 * 1024
        ),
        name="forecast",
    )(
        *(
            pltpu.with_memory_space_constraint(x, pltpu.HBM)
            for x in (
                jnp.swapaxes(coupling_index, 1, 2), input_index, region_band,
                field_state, reservoir_state, coupling_blocks, input_blocks, readout,
            )
        )
    )
    return pl.pallas_call(
        deliver,
        out_shape=(
            jax.ShapeDtypeStruct(field_state.shape, BF16),
            jax.ShapeDtypeStruct(reservoir_state.shape, BF16),
        ),
        in_specs=[vmem] * 2,
        out_specs=(hbm, hbm),
        scratch_shapes=[pltpu.SemaphoreType.DMA((2,))],
        compiler_params=pltpu.CompilerParams(vmem_limit_bytes=32 * 1024 * 1024),
        name="deliver",
    )(*(pltpu.with_memory_space_constraint(x, pltpu.VMEM) for x in (field, state)))


def solution(mesh):
    return jax.shard_map(
        per_device,
        mesh=mesh,
        in_specs=(
            P(None, "lat", "lon"),
            P("lat", "lon", None, None),
            P("lat", None, None),
            P("lat", None, None),
            P("lat", None, None),
            P("lat", None),
            P("lat", None, None),
            P("lat"),
        ),
        out_specs=(P(None, "lat", "lon"), P("lat", "lon", None, None)),
        check_vma=False,
    )
```

```python
import functools

import jax
import jax.numpy as jnp
from jax import lax
from jax.experimental import pallas as pl
from jax.experimental.pallas import tpu as pltpu
from jax.sharding import PartitionSpec as P

MESH = pl.DeviceIdType.MESH
STEPS = 3
F32 = jnp.float32
BF16 = jnp.bfloat16
TILES = 10
ROWS = 8 * TILES

DIRS = ((-1, 0), (1, 0), (0, -1), (0, 1), (-1, -1), (-1, 1), (1, -1), (1, 1))


def dot_nt(x, w):
    return lax.dot_general(x, w, (((1,), (1,)), ((), ())), preferred_element_type=F32)


def row_of(column, member):
    at = column + 2
    return at % TILES * 8 + at // TILES * 4 + member


def dot_nn(x, w):
    return lax.dot_general(x, w, (((1,), (0,)), ((), ())), preferred_element_type=F32)


def lanes(rows):
    return lax.broadcasted_iota(jnp.int32, (rows, 128), 1)


def roll(x, by):
    return pltpu.roll(x, by, 1)


def minus_parts(r0, r1, r2):
    lane = lanes(r0.shape[0])
    b0 = jnp.where(lane < 48, roll(r0, 48), roll(r1, 48))
    r2r = roll(r2, 80)
    b2 = jnp.where(lane < 80, roll(r1, 80), r2r)
    return b0, b2, r2r


def plus_parts(r0, r1):
    r0r = roll(r0, 112)
    return r0r, r0r, roll(r1, 16)


def windows(r0, r1, r2, n):
    rows = 8 * n
    lane = lanes(rows)
    m = slice(0, rows)
    c = slice(8, rows + 8)
    p = slice(16, rows + 16)
    m0, m2, m3 = minus_parts(r0[m], r1[m], r2[m])
    p1, p2, p4 = plus_parts(r0[p], r1[p])
    c0 = roll(r0[c], 80)
    c1 = roll(r1[c], 80)
    d1 = roll(r1[c], 112)
    d2 = roll(r2[c], 112)
    b0 = jnp.where(lane < 80, m0, c0)
    b1 = jnp.where(lane < 80, c0, jnp.where(lane < 112, c1, p1))
    b2 = jnp.where(lane < 64, p2, m2)
    b3 = jnp.where(lane < 16, m3, jnp.where(lane < 112, d1, d2))
    b4 = jnp.where(lane < 48, d2, p4)
    return b0, b1, b2, b3, b4


def kernel(
    cidx_hbm, qidx_hbm, rband_hbm,
    field_hbm, state_hbm, coup_hbm, drive_hbm, read_hbm,
    field_out, state_out,
    cidx, qidx, rband,
    field_in, state_in, coup, drive, read, drive_t, read_t,
    states, pre, win, raw, halo, edge, edge_in, state_edge, ta, tb, ea, eb,
    local_sem, send_sem, recv_sem, ready,
):
    lat, lon = lax.axis_index("lat"), lax.axis_index("lon")
    nlat, nlon = lax.axis_size("lat"), lax.axis_size("lon")
    west, east = lax.rem(lon + nlon - 1, nlon), lax.rem(lon + 1, nlon)
    has_south = lat > 0
    has_north = lat < nlat - 1

    def target(d):
        dl, do = DIRS[d]
        return (lat + dl, west if do < 0 else (east if do > 0 else lon))

    def by_side(fn, dirs=range(8)):
        for d in dirs:
            dl = DIRS[d][0]
            if dl == 0:
                fn(d)
            else:
                pl.when(has_south if dl < 0 else has_north)(functools.partial(fn, d))

    loads = [
        pltpu.make_async_copy(src, dst, local_sem.at[n])
        for n, (src, dst) in enumerate(
            ((field_hbm.at[:, :, 2048:2560], field_in.at[:, :, 2048:2560]),
             (field_hbm.at[:, :, 0:2048], field_in.at[:, :, 0:2048]),
             (state_hbm, state_in), (coup_hbm, coup), (drive_hbm, drive), (read_hbm, read),
             (cidx_hbm, cidx), (qidx_hbm, qidx), (rband_hbm, rband))
        )
    ]
    loads[0].start()

    is_first = lon == 0
    is_last = lon == nlon - 1
    is_before_last = lon == nlon - 2
    greeted = 1 + has_south.astype(jnp.int32) + has_north.astype(jnp.int32)

    barrier = pltpu.get_barrier_semaphore()

    def greet(d):
        pl.semaphore_signal(barrier, inc=1, device_id=target(d), device_id_type=MESH)

    by_side(greet, (4, 6, 2))

    @pl.when(jnp.logical_not(is_last))
    def _():
        by_side(greet, (0, 1))
        pl.when(jnp.logical_not(is_before_last))(lambda: by_side(greet, (5, 7, 3)))

    for load in loads[1:]:
        load.start()

    def remote(src, dst, step, n, d):
        return pltpu.make_async_remote_copy(
            src_ref=src, dst_ref=dst, send_sem=send_sem.at[step, n], recv_sem=recv_sem.at[step, n],
            device_id=target(d), device_id_type=MESH,
        )

    def message(step, d):
        if d == 0:
            return remote(raw.at[step, 0], halo.at[step, 1], step, d, d)
        if d == 1:
            return remote(raw.at[step, 3], halo.at[step, 0], step, d, d)
        dl, do = DIRS[d]
        side, into = (0, 1) if do < 0 else (1, 0)
        if dl == 0:
            return remote(edge.at[side], edge_in.at[into], step, d, d)
        pair = 0 if dl < 0 else 3
        return remote(edge.at[side, pair], edge_in.at[2 + into, pair], step, d, d)

    def state_message(d):
        side, into = (0, 1) if DIRS[d][1] < 0 else (1, 0)
        return remote(state_hbm.at[:, pl.ds(14 * side, 2)], state_edge.at[into], 0, 6 + d, d)

    def wait_recv(step, dirs):
        for d in dirs:
            dl = DIRS[d][0]
            if dl == 0:
                message(step, d).wait_recv()
            else:
                pl.when(has_north if dl < 0 else has_south)(message(step, d).wait_recv)

    def put_raw(step, pair, r):
        for k in range(3):
            raw[step, pair, k] = r[k].astype(BF16)

    @pl.when(is_last)
    def _():
        pl.semaphore_wait(barrier, greeted)
        state_message(3).start()

    lane8 = lanes(8)

    def to_regions(columns, row, stride, to_a, to_b):
        for m in range(4):
            f = {}
            for j in columns:
                q, off = (160 * j) // 128, (160 * j) % 128
                for k in (q, q + 1):
                    if k not in f:
                        f[k] = field_in[m, :, 128 * k:128 * (k + 1)].astype(F32)
                if off == 0:
                    w0, w1 = f[q], f[q + 1]
                else:
                    w1 = roll(f[q + 1], 128 - off)
                    w0 = jnp.where(lane8 < 128 - off, roll(f[q], 128 - off), w1)
                to_a[pl.ds(row(j, m), 8, stride=stride), :] = w0
                to_b[pl.ds(row(j, m), 8, stride=stride), :] = w1

    def to_pair(p, rows, from_a, from_b):
        lane = lanes(rows)
        lo, mid, hi = 2 * p * rows, (2 * p + 1) * rows, (2 * p + 2) * rows
        a0, a1 = from_a[lo:mid], from_b[lo:mid]
        b0, b1 = roll(from_a[mid:hi], 32), roll(from_b[mid:hi], 32)
        return a0, jnp.where(lane < 32, a1, b0), jnp.where(lane < 32, b0, b1)

    def put_edge(side, first):
        to_regions(range(first, first + 3), lambda j, m: 4 * (j - first) + m, 16, ea.at[side], eb.at[side])
        for p in range(4):
            for k, rows in enumerate(to_pair(p, 16, ea.at[side], eb.at[side])):
                edge[side, p, k] = rows.astype(BF16)

    def start(d):
        message(0, d).start()

    loads[0].wait()
    put_edge(1, 13)
    pl.when(is_last)(lambda: by_side(start, (5, 7, 3)))
    loads[1].wait()
    put_edge(0, 0)
    to_regions(range(16), row_of, ROWS, ta, tb)
    for p in range(4):
        put_raw(0, p, to_pair(p, ROWS, ta, tb))

    @pl.when(lat == 0)
    def _():
        halo[:, 0] = jnp.zeros(halo.shape[:1] + halo.shape[2:], BF16)
        edge_in[2:4, 3] = jnp.zeros((2,) + edge_in.shape[2:], BF16)

    @pl.when(lat == nlat - 1)
    def _():
        halo[:, 1] = jnp.zeros(halo.shape[:1] + halo.shape[2:], BF16)
        edge_in[2:4, 0] = jnp.zeros((2,) + edge_in.shape[2:], BF16)

    def send_west():
        by_side(start, (4, 6, 2))
        state_message(2).start()

    @pl.when(is_last)
    def _():
        pl.semaphore_wait(ready, 1)
        by_side(start, (0, 1))
        send_west()

    @pl.when(jnp.logical_not(is_last))
    def _():
        pl.semaphore_wait(barrier, 2 * greeted - 1 + jnp.where(is_first, 0, greeted))

        @pl.when(is_before_last)
        def _():
            pl.semaphore_signal(ready, inc=1, device_id=(lat, east), device_id_type=MESH)

        by_side(start, (5, 7, 3))
        state_message(3).start()
        by_side(start, (0, 1))
        pl.when(jnp.logical_not(is_first))(send_west)

    def put_state(i, t):
        tiles = []
        for s in (t, t + 1):
            tiles.append(state_in[i, s - 2] if s >= 2 else state_edge[0, i, s])
            tiles.append(state_in[i, s + 8] if s < 8 else state_edge[1, i, s - 8])
        rows = jnp.concatenate([x.astype(F32) for x in tiles], axis=0).astype(BF16)
        for c in range(8):
            states[c, ROWS * i + 8 * t:ROWS * i + 8 * t + 16] = rows[:, 128 * c:128 * (c + 1)]

    loads[2].wait()
    for i in range(2):
        for t in (2, 4, 6):
            put_state(i, t)
    for load in loads[3:]:
        load.wait()
    bands = [rband[i] for i in range(2)]

    for band in range(2):
        for b in range(8):
            drive_t[band, 128 * b:128 * (b + 1)] = drive[band, 128 * b:128 * (b + 1)].T
    for h in range(2):
        for c in range(8):
            part = read[0, 320 * h:320 * h + 320, 128 * c:128 * (c + 1)]
            part = jnp.concatenate([part, jnp.zeros((64, 128), BF16)], axis=0)
            read_t[h, 128 * c:128 * (c + 1)] = part.T

    def put_windows(at, ext):
        for k, block in enumerate(windows(*ext, TILES)):
            win[at + k] = block.astype(BF16)

    def western(r, w):
        return jnp.concatenate(
            [w[0:4], r[72:76], w[4:8], r[4:8], w[8:12], r[12:16], r[16:40]], axis=0
        )

    def eastern(r, x):
        return jnp.concatenate(
            [r[24:64], r[64:68], x[0:4], r[72:76], x[4:8], r[4:8], x[8:12]], axis=0
        )

    starts = [(5 + 5 * p, raw.at[0, p], 0, p) for p in range(4)]
    starts += [(0, halo.at[0, 0], 2, 3), (25, halo.at[0, 1], 2, 0)]

    def put_start_windows(pairs, side, tiles, at, rows):
        for to, ref, edges, p in pairs:
            ext = [tiles(ref[k].astype(F32), edge_in[edges + side, p, k].astype(F32)) for k in range(3)]
            for k, block in enumerate(windows(*ext, rows // 8)):
                win[to + k, at:at + rows] = block.astype(BF16)

    def without_edges(r):
        return jnp.concatenate([r[72:76], r[72:76], r, r[4:8], r[4:8]], axis=0)

    near = jnp.where(lat < nlat // 2, 0, 1)
    for step in range(STEPS):
        if step == 0:
            state_message(2).wait_recv()
            for i in range(2):
                put_state(i, 8)
            wait_recv(step, (2,))
            put_start_windows(starts[:4], 1, eastern, 32, 48)
            wait_recv(step, (0, 1, 4, 6))
            put_start_windows(starts[4:], 1, eastern, 32, 48)
            state_message(3).wait_recv()
            for i in range(2):
                put_state(i, 0)
        for i in range(2):
            for b in range(8):
                x = jnp.concatenate(
                    [states[cidx[bands[i], k, b], ROWS * i:ROWS * (i + 1)] for k in range(2)], axis=1
                )
                w = jnp.concatenate(
                    [coup[bands[i], (2 * b + k) * 128:(2 * b + k + 1) * 128] for k in range(2)], axis=1
                )
                pre[i, b] = dot_nt(x, w)
        if step == 0:
            wait_recv(step, (3, 5, 7))
            put_start_windows(starts, 0, western, 0, 32)
        else:
            for p in range(4):
                put_windows(5 + 5 * p, [without_edges(raw[step, p, k].astype(F32)) for k in range(3)])

        def put_halo_windows(i):
            put_windows(25 * i, [without_edges(halo[step, i, k].astype(F32)) for k in range(3)])

        def put_new_states(i):
            band = rband[i]
            rows = pl.ds(pl.multiple_of(ROWS * i, ROWS), ROWS)
            for b in range(8):
                x = win[10 * i + qidx[band, b]]
                w = drive_t[band, 128 * b:128 * (b + 1)]
                new = jnp.tanh(pre[i, b] + dot_nn(x, w))
                states[b, rows] = new.astype(BF16)
                if step == STEPS - 1:
                    for j in range(16):
                        at = row_of(j, 0)
                        state_out[i, j, :, 128 * b:128 * (b + 1)] = new[at:at + 4].astype(BF16)

        if step == 0:
            for i in range(2):
                put_new_states(i)
        else:
            for n in range(2):
                i = near if n == 0 else 1 - near
                pl.when((i == 0) & has_south)(message(step, 1).wait_recv)
                pl.when((i == 1) & has_north)(message(step, 0).wait_recv)
                put_halo_windows(i)
                put_new_states(i)
        x = jnp.concatenate([states[c] for c in range(8)], axis=1)
        if step < STEPS - 1:
            first = 1 - near
            for n in range(2):
                h = first if n == 0 else 1 - first
                y = dot_nn(x, read_t[h])
                for i in range(2):
                    put_raw(
                        step + 1, 2 * i + h,
                        tuple(y[ROWS * i:ROWS * (i + 1), 128 * k:128 * (k + 1)] for k in range(3)),
                    )
                pl.when((h == 0) & has_south)(message(step + 1, 0).start)
                pl.when((h == 1) & has_north)(message(step + 1, 1).start)
            if step == 0:
                pl.when(is_first)(send_west)
        else:
            lane = lanes(ROWS)
            for h in range(2):
                y = dot_nn(x, read_t[h])
                for i in range(2):
                    y0, y1, y2 = (y[ROWS * i:ROWS * (i + 1), 128 * k:128 * (k + 1)] for k in range(3))
                    at = ROWS * (4 * i + 2 * h)
                    ta[at:at + ROWS] = y0
                    tb[at:at + ROWS] = y1
                    r1, r2 = roll(y1, 96), roll(y2, 96)
                    ta[at + ROWS:at + 2 * ROWS] = jnp.where(lane < 96, r1, r2)
                    tb[at + ROWS:at + 2 * ROWS] = r2

    for m in range(4):
        cols = []
        prev = None
        for j in range(16):
            off = (160 * j) % 128
            v0 = ta[pl.ds(row_of(j, m), 8, stride=ROWS), :]
            v1 = tb[pl.ds(row_of(j, m), 8, stride=ROWS), :]
            if off == 0:
                cols.append(v0)
                prev = (v0, v1, 0)
                continue
            r0, r1 = roll(v0, off), roll(v1, off)
            p0, p1, po = prev
            cols.append(jnp.where(lane8 < po, p0, jnp.where(lane8 < po + 32, p1, r0)))
            prev = (r0, r1, off)
            if off == 96:
                cols.append(jnp.where(lane8 < 96, r0, r1))
        for k in range(20):
            field_out[m, :, 128 * k:128 * (k + 1)] = cols[k].astype(BF16)

    by_side(lambda d: message(0, d).wait_send())
    for d in (2, 3):
        state_message(d).wait_send()
    for step in range(1, STEPS):
        by_side(lambda d: message(step, d).wait_send(), (0, 1))


def deliver(field_ref, state_ref, field_out, state_out, sems):
    copies = [
        pltpu.make_async_copy(field_ref, field_out, sems.at[0]),
        pltpu.make_async_copy(state_ref, state_out, sems.at[1]),
    ]
    for copy in copies:
        copy.start()
    for copy in copies:
        copy.wait()


def per_device(field_state, reservoir_state, coupling_blocks, coupling_index, input_blocks, input_index, readout, region_band):
    hbm = pl.BlockSpec(memory_space=pltpu.HBM)
    vmem = pl.BlockSpec(memory_space=pltpu.VMEM)
    field, state = pl.pallas_call(
        kernel,
        out_shape=(
            pltpu.VMEM(field_state.shape, BF16),
            pltpu.VMEM(reservoir_state.shape, BF16),
        ),
        in_specs=[hbm] * 8,
        out_specs=(vmem, vmem),
        scratch_shapes=[
            pltpu.SMEM((2, 2, 8), jnp.int32),
            pltpu.SMEM((2, 8), jnp.int32),
            pltpu.SMEM((2,), jnp.int32),
            pltpu.VMEM(field_state.shape, BF16),
            pltpu.VMEM(reservoir_state.shape, BF16),
            pltpu.VMEM(coupling_blocks.shape, BF16),
            pltpu.VMEM(input_blocks.shape, BF16),
            pltpu.VMEM(readout.shape, BF16),
            pltpu.VMEM(input_blocks.shape, BF16),
            pltpu.VMEM((2, 1024, 384), BF16),
            pltpu.VMEM((8, 2 * ROWS, 128), BF16),
            pltpu.VMEM((2, 8, ROWS, 128), F32),
            pltpu.VMEM((30, ROWS, 128), BF16),
            pltpu.VMEM((STEPS, 4, 3, ROWS, 128), BF16),
            pltpu.VMEM((STEPS, 2, 3, ROWS, 128), BF16),
            pltpu.VMEM((2, 4, 3, 16, 128), BF16),
            pltpu.VMEM((4, 4, 3, 16, 128), BF16),
            pltpu.VMEM((2, 2, 2, 4, 1024), BF16),
            pltpu.VMEM((8 * ROWS, 128), F32),
            pltpu.VMEM((8 * ROWS, 128), F32),
            pltpu.VMEM((2, 128, 128), F32),
            pltpu.VMEM((2, 128, 128), F32),
            pltpu.SemaphoreType.DMA((9,)),
            pltpu.SemaphoreType.DMA((STEPS, 10)),
            pltpu.SemaphoreType.DMA((STEPS, 10)),
            pltpu.SemaphoreType.REGULAR,
        ],
        compiler_params=pltpu.CompilerParams(
            collective_id=0, has_side_effects=True, vmem_limit_bytes=32 * 1024 * 1024
        ),
        name="forecast",
    )(
        *(
            pltpu.with_memory_space_constraint(x, pltpu.HBM)
            for x in (
                jnp.swapaxes(coupling_index, 1, 2), input_index, region_band,
                field_state, reservoir_state, coupling_blocks, input_blocks, readout,
            )
        )
    )
    return pl.pallas_call(
        deliver,
        out_shape=(
            jax.ShapeDtypeStruct(field_state.shape, BF16),
            jax.ShapeDtypeStruct(reservoir_state.shape, BF16),
        ),
        in_specs=[vmem] * 2,
        out_specs=(hbm, hbm),
        scratch_shapes=[pltpu.SemaphoreType.DMA((2,))],
        compiler_params=pltpu.CompilerParams(vmem_limit_bytes=32 * 1024 * 1024),
        name="deliver",
    )(*(pltpu.with_memory_space_constraint(x, pltpu.VMEM) for x in (field, state)))


def solution(mesh):
    return jax.shard_map(
        per_device,
        mesh=mesh,
        in_specs=(
            P(None, "lat", "lon"),
            P("lat", "lon", None, None),
            P("lat", None, None),
            P("lat", None, None),
            P("lat", None, None),
            P("lat", None),
            P("lat", None, None),
            P("lat"),
        ),
        out_specs=(P(None, "lat", "lon"), P("lat", "lon", None, None)),
        check_vma=False,
    )
```

```python
import functools

import jax
import jax.numpy as jnp
from jax import lax
from jax.experimental import pallas as pl
from jax.experimental.pallas import tpu as pltpu
from jax.sharding import PartitionSpec as P

MESH = pl.DeviceIdType.MESH
STEPS = 3
F32 = jnp.float32
BF16 = jnp.bfloat16
TILES = 10
ROWS = 8 * TILES

DIRS = ((-1, 0), (1, 0), (0, -1), (0, 1), (-1, -1), (-1, 1), (1, -1), (1, 1))


def dot_nt(x, w):
    return lax.dot_general(x, w, (((1,), (1,)), ((), ())), preferred_element_type=F32)


def row_of(column, member):
    at = column + 2
    return at % TILES * 8 + at // TILES * 4 + member


def dot_nn(x, w):
    return lax.dot_general(x, w, (((1,), (0,)), ((), ())), preferred_element_type=F32)


def lanes(rows):
    return lax.broadcasted_iota(jnp.int32, (rows, 128), 1)


def roll(x, by):
    return pltpu.roll(x, by, 1)


def minus_parts(r0, r1, r2):
    lane = lanes(r0.shape[0])
    b0 = jnp.where(lane < 48, roll(r0, 48), roll(r1, 48))
    r2r = roll(r2, 80)
    b2 = jnp.where(lane < 80, roll(r1, 80), r2r)
    return b0, b2, r2r


def plus_parts(r0, r1):
    r0r = roll(r0, 112)
    return r0r, r0r, roll(r1, 16)


def windows(r0, r1, r2, n):
    rows = 8 * n
    lane = lanes(rows)
    m = slice(0, rows)
    c = slice(8, rows + 8)
    p = slice(16, rows + 16)
    m0, m2, m3 = minus_parts(r0[m], r1[m], r2[m])
    p1, p2, p4 = plus_parts(r0[p], r1[p])
    c0 = roll(r0[c], 80)
    c1 = roll(r1[c], 80)
    d1 = roll(r1[c], 112)
    d2 = roll(r2[c], 112)
    b0 = jnp.where(lane < 80, m0, c0)
    b1 = jnp.where(lane < 80, c0, jnp.where(lane < 112, c1, p1))
    b2 = jnp.where(lane < 64, p2, m2)
    b3 = jnp.where(lane < 16, m3, jnp.where(lane < 112, d1, d2))
    b4 = jnp.where(lane < 48, d2, p4)
    return b0, b1, b2, b3, b4


def kernel(
    cidx_hbm, qidx_hbm, rband_hbm,
    field_hbm, state_hbm, coup_hbm, drive_hbm, read_hbm,
    field_out, state_out,
    cidx, qidx, rband,
    field_in, state_in, coup, drive, read, drive_t, read_t,
    states, pre, win, raw, halo, edge, edge_in, state_edge, ta, tb, ea, eb,
    local_sem, send_sem, recv_sem, ready,
):
    lat, lon = lax.axis_index("lat"), lax.axis_index("lon")
    nlat, nlon = lax.axis_size("lat"), lax.axis_size("lon")
    west, east = lax.rem(lon + nlon - 1, nlon), lax.rem(lon + 1, nlon)
    has_south = lat > 0
    has_north = lat < nlat - 1

    def target(d):
        dl, do = DIRS[d]
        return (lat + dl, west if do < 0 else (east if do > 0 else lon))

    def by_side(fn, dirs=range(8)):
        for d in dirs:
            dl = DIRS[d][0]
            if dl == 0:
                fn(d)
            else:
                pl.when(has_south if dl < 0 else has_north)(functools.partial(fn, d))

    loads = [
        pltpu.make_async_copy(src, dst, local_sem.at[n])
        for n, (src, dst) in enumerate(
            ((field_hbm.at[:, :, 2048:2560], field_in.at[:, :, 2048:2560]),
             (field_hbm.at[:, :, 0:2048], field_in.at[:, :, 0:2048]),
             (state_hbm, state_in), (coup_hbm, coup), (drive_hbm, drive), (read_hbm, read),
             (cidx_hbm, cidx), (qidx_hbm, qidx), (rband_hbm, rband))
        )
    ]
    loads[0].start()

    is_first = lon == 0
    is_last = lon == nlon - 1
    is_before_last = lon == nlon - 2
    greeted = 1 + has_south.astype(jnp.int32) + has_north.astype(jnp.int32)

    barrier = pltpu.get_barrier_semaphore()

    def greet(d):
        pl.semaphore_signal(barrier, inc=1, device_id=target(d), device_id_type=MESH)

    by_side(greet, (4, 6, 2))

    @pl.when(jnp.logical_not(is_last))
    def _():
        by_side(greet, (0, 1))
        pl.when(jnp.logical_not(is_before_last))(lambda: by_side(greet, (5, 7, 3)))

    for load in loads[1:]:
        load.start()

    def remote(src, dst, step, n, d):
        return pltpu.make_async_remote_copy(
            src_ref=src, dst_ref=dst, send_sem=send_sem.at[step, n], recv_sem=recv_sem.at[step, n],
            device_id=target(d), device_id_type=MESH,
        )

    def message(step, d):
        if d == 0:
            return remote(raw.at[step, 0], halo.at[step, 1], step, d, d)
        if d == 1:
            return remote(raw.at[step, 3], halo.at[step, 0], step, d, d)
        dl, do = DIRS[d]
        side, into = (0, 1) if do < 0 else (1, 0)
        if dl == 0:
            return remote(edge.at[side], edge_in.at[into], step, d, d)
        pair = 0 if dl < 0 else 3
        return remote(edge.at[side, pair], edge_in.at[2 + into, pair], step, d, d)

    def lat_part(step, d, n):
        pair, side = (0, 1) if d == 0 else (3, 0)
        blocks = pl.ds(2 * n, 2 - n)
        return remote(raw.at[step, pair, blocks], halo.at[step, side, blocks], step, d + 4 * n, d)

    def state_message(d):
        side, into = (0, 1) if DIRS[d][1] < 0 else (1, 0)
        return remote(state_hbm.at[:, pl.ds(14 * side, 2)], state_edge.at[into], 0, 6 + d, d)

    def wait_recv(step, dirs):
        for d in dirs:
            dl = DIRS[d][0]
            if dl == 0:
                message(step, d).wait_recv()
            else:
                pl.when(has_north if dl < 0 else has_south)(message(step, d).wait_recv)

    def put_raw(step, pair, r):
        for k in range(3):
            raw[step, pair, k] = r[k].astype(BF16)

    @pl.when(is_last)
    def _():
        pl.semaphore_wait(barrier, greeted)
        state_message(3).start()

    lane8 = lanes(8)

    def to_regions(columns, row, stride, to_a, to_b):
        for m in range(4):
            f = {}
            for j in columns:
                q, off = (160 * j) // 128, (160 * j) % 128
                for k in (q, q + 1):
                    if k not in f:
                        f[k] = field_in[m, :, 128 * k:128 * (k + 1)].astype(F32)
                if off == 0:
                    w0, w1 = f[q], f[q + 1]
                else:
                    w1 = roll(f[q + 1], 128 - off)
                    w0 = jnp.where(lane8 < 128 - off, roll(f[q], 128 - off), w1)
                to_a[pl.ds(row(j, m), 8, stride=stride), :] = w0
                to_b[pl.ds(row(j, m), 8, stride=stride), :] = w1

    def to_pair(p, rows, from_a, from_b):
        lane = lanes(rows)
        lo, mid, hi = 2 * p * rows, (2 * p + 1) * rows, (2 * p + 2) * rows
        a0, a1 = from_a[lo:mid], from_b[lo:mid]
        b0, b1 = roll(from_a[mid:hi], 32), roll(from_b[mid:hi], 32)
        return a0, jnp.where(lane < 32, a1, b0), jnp.where(lane < 32, b0, b1)

    def put_edge(side, first):
        to_regions(range(first, first + 3), lambda j, m: 4 * (j - first) + m, 16, ea.at[side], eb.at[side])
        for p in range(4):
            for k, rows in enumerate(to_pair(p, 16, ea.at[side], eb.at[side])):
                edge[side, p, k] = rows.astype(BF16)

    def start(d):
        message(0, d).start()

    loads[0].wait()
    put_edge(1, 13)
    pl.when(is_last)(lambda: by_side(start, (5, 7, 3)))
    loads[1].wait()
    put_edge(0, 0)
    to_regions(range(16), row_of, ROWS, ta, tb)
    for p in range(4):
        put_raw(0, p, to_pair(p, ROWS, ta, tb))

    @pl.when(lat == 0)
    def _():
        halo[:, 0] = jnp.zeros(halo.shape[:1] + halo.shape[2:], BF16)
        edge_in[2:4, 3] = jnp.zeros((2,) + edge_in.shape[2:], BF16)

    @pl.when(lat == nlat - 1)
    def _():
        halo[:, 1] = jnp.zeros(halo.shape[:1] + halo.shape[2:], BF16)
        edge_in[2:4, 0] = jnp.zeros((2,) + edge_in.shape[2:], BF16)

    def send_west():
        by_side(start, (4, 6, 2))
        state_message(2).start()

    @pl.when(is_last)
    def _():
        pl.semaphore_wait(ready, 1)
        by_side(start, (0, 1))
        send_west()

    @pl.when(jnp.logical_not(is_last))
    def _():
        pl.semaphore_wait(barrier, 2 * greeted - 1 + jnp.where(is_first, 0, greeted))

        @pl.when(is_before_last)
        def _():
            pl.semaphore_signal(ready, inc=1, device_id=(lat, east), device_id_type=MESH)

        by_side(start, (5, 7, 3))
        state_message(3).start()
        by_side(start, (0, 1))
        pl.when(jnp.logical_not(is_first))(send_west)

    def put_state(i, t):
        tiles = []
        for s in (t, t + 1):
            tiles.append(state_in[i, s - 2] if s >= 2 else state_edge[0, i, s])
            tiles.append(state_in[i, s + 8] if s < 8 else state_edge[1, i, s - 8])
        rows = jnp.concatenate([x.astype(F32) for x in tiles], axis=0).astype(BF16)
        for c in range(8):
            states[c, ROWS * i + 8 * t:ROWS * i + 8 * t + 16] = rows[:, 128 * c:128 * (c + 1)]

    loads[2].wait()
    for i in range(2):
        for t in (2, 4, 6):
            put_state(i, t)
    for load in loads[3:]:
        load.wait()
    bands = [rband[i] for i in range(2)]

    for band in range(2):
        for b in range(8):
            drive_t[band, 128 * b:128 * (b + 1)] = drive[band, 128 * b:128 * (b + 1)].T
    for h in range(2):
        for c in range(8):
            part = read[0, 320 * h:320 * h + 320, 128 * c:128 * (c + 1)]
            part = jnp.concatenate([part, jnp.zeros((64, 128), BF16)], axis=0)
            read_t[h, 128 * c:128 * (c + 1)] = part.T

    def put_windows(at, ext):
        for k, block in enumerate(windows(*ext, TILES)):
            win[at + k] = block.astype(BF16)

    def western(r, w):
        return jnp.concatenate(
            [w[0:4], r[72:76], w[4:8], r[4:8], w[8:12], r[12:16], r[16:40]], axis=0
        )

    def eastern(r, x):
        return jnp.concatenate(
            [r[24:64], r[64:68], x[0:4], r[72:76], x[4:8], r[4:8], x[8:12]], axis=0
        )

    starts = [(5 + 5 * p, raw.at[0, p], 0, p) for p in range(4)]
    starts += [(0, halo.at[0, 0], 2, 3), (25, halo.at[0, 1], 2, 0)]

    def put_start_windows(pairs, side, tiles, at, rows):
        for to, ref, edges, p in pairs:
            ext = [tiles(ref[k].astype(F32), edge_in[edges + side, p, k].astype(F32)) for k in range(3)]
            for k, block in enumerate(windows(*ext, rows // 8)):
                win[to + k, at:at + rows] = block.astype(BF16)

    def without_edges(r):
        return jnp.concatenate([r[72:76], r[72:76], r, r[4:8], r[4:8]], axis=0)

    near = jnp.where(lat < nlat // 2, 0, 1)
    for step in range(STEPS):
        if step == 0:
            state_message(2).wait_recv()
            for i in range(2):
                put_state(i, 8)
            wait_recv(step, (2,))
            put_start_windows(starts[:4], 1, eastern, 32, 48)
            wait_recv(step, (0, 1, 4, 6))
            put_start_windows(starts[4:], 1, eastern, 32, 48)
            state_message(3).wait_recv()
            for i in range(2):
                put_state(i, 0)
        for i in range(2):
            for b in range(8):
                x = jnp.concatenate(
                    [states[cidx[bands[i], k, b], ROWS * i:ROWS * (i + 1)] for k in range(2)], axis=1
                )
                w = jnp.concatenate(
                    [coup[bands[i], (2 * b + k) * 128:(2 * b + k + 1) * 128] for k in range(2)], axis=1
                )
                pre[i, b] = dot_nt(x, w)
        if step == 0:
            wait_recv(step, (3, 5, 7))
            put_start_windows(starts, 0, western, 0, 32)
        else:
            for p in range(4):
                put_windows(5 + 5 * p, [without_edges(raw[step, p, k].astype(F32)) for k in range(3)])

        def put_halo_windows(i):
            put_windows(25 * i, [without_edges(halo[step, i, k].astype(F32)) for k in range(3)])

        def put_new_states(i):
            band = rband[i]
            rows = pl.ds(pl.multiple_of(ROWS * i, ROWS), ROWS)
            for b in range(8):
                x = win[10 * i + qidx[band, b]]
                w = drive_t[band, 128 * b:128 * (b + 1)]
                new = jnp.tanh(pre[i, b] + dot_nn(x, w))
                states[b, rows] = new.astype(BF16)
                if step == STEPS - 1:
                    for j in range(16):
                        at = row_of(j, 0)
                        state_out[i, j, :, 128 * b:128 * (b + 1)] = new[at:at + 4].astype(BF16)

        if step == 0:
            for i in range(2):
                put_new_states(i)
        else:
            for turn in range(2):
                i = near if turn == 0 else 1 - near
                for n in range(2):
                    pl.when((i == 0) & has_south)(lat_part(step, 1, n).wait_recv)
                    pl.when((i == 1) & has_north)(lat_part(step, 0, n).wait_recv)
                put_halo_windows(i)
                put_new_states(i)
        x = jnp.concatenate([states[c] for c in range(8)], axis=1)
        if step < STEPS - 1:
            far = 1 - near

            def put(i, h, y, first=0):
                for k in range(y.shape[1] // 128):
                    raw[step + 1, 2 * i + h, first + k] = y[:, 128 * k:128 * (k + 1)].astype(BF16)

            def go(h, parts):
                for n in parts:
                    pl.when((h == 0) & has_south)(lat_part(step + 1, 0, n).start)
                    pl.when((h == 1) & has_north)(lat_part(step + 1, 1, n).start)

            far_rows = pl.ds(pl.multiple_of(ROWS * far, ROWS), ROWS)
            x_far = jnp.concatenate([states[c, far_rows] for c in range(8)], axis=1)
            put(far, far, dot_nn(x_far, read_t[far, :, 0:256]))
            go(far, (0,))
            put(far, far, dot_nn(x_far, read_t[far, :, 256:384]), 2)
            go(far, (1,))
            y = dot_nn(x, read_t[near])
            for i in range(2):
                put(i, near, y[ROWS * i:ROWS * (i + 1)])
            go(near, (0, 1))
            near_rows = pl.ds(pl.multiple_of(ROWS * near, ROWS), ROWS)
            x_near = jnp.concatenate([states[c, near_rows] for c in range(8)], axis=1)
            put(near, far, dot_nn(x_near, read_t[far]))
            if step == 0:
                pl.when(is_first)(send_west)
        else:
            lane = lanes(ROWS)
            for h in range(2):
                y = dot_nn(x, read_t[h])
                for i in range(2):
                    y0, y1, y2 = (y[ROWS * i:ROWS * (i + 1), 128 * k:128 * (k + 1)] for k in range(3))
                    at = ROWS * (4 * i + 2 * h)
                    ta[at:at + ROWS] = y0
                    tb[at:at + ROWS] = y1
                    r1, r2 = roll(y1, 96), roll(y2, 96)
                    ta[at + ROWS:at + 2 * ROWS] = jnp.where(lane < 96, r1, r2)
                    tb[at + ROWS:at + 2 * ROWS] = r2

    for m in range(4):
        cols = []
        prev = None
        for j in range(16):
            off = (160 * j) % 128
            v0 = ta[pl.ds(row_of(j, m), 8, stride=ROWS), :]
            v1 = tb[pl.ds(row_of(j, m), 8, stride=ROWS), :]
            if off == 0:
                cols.append(v0)
                prev = (v0, v1, 0)
                continue
            r0, r1 = roll(v0, off), roll(v1, off)
            p0, p1, po = prev
            cols.append(jnp.where(lane8 < po, p0, jnp.where(lane8 < po + 32, p1, r0)))
            prev = (r0, r1, off)
            if off == 96:
                cols.append(jnp.where(lane8 < 96, r0, r1))
        for k in range(20):
            field_out[m, :, 128 * k:128 * (k + 1)] = cols[k].astype(BF16)

    by_side(lambda d: message(0, d).wait_send())
    for d in (2, 3):
        state_message(d).wait_send()
    for step in range(1, STEPS):
        for n in range(2):
            by_side(lambda d: lat_part(step, d, n).wait_send(), (0, 1))


def deliver(field_ref, state_ref, field_out, state_out, sems):
    copies = [
        pltpu.make_async_copy(field_ref, field_out, sems.at[0]),
        pltpu.make_async_copy(state_ref, state_out, sems.at[1]),
    ]
    for copy in copies:
        copy.start()
    for copy in copies:
        copy.wait()


def per_device(field_state, reservoir_state, coupling_blocks, coupling_index, input_blocks, input_index, readout, region_band):
    hbm = pl.BlockSpec(memory_space=pltpu.HBM)
    vmem = pl.BlockSpec(memory_space=pltpu.VMEM)
    field, state = pl.pallas_call(
        kernel,
        out_shape=(
            pltpu.VMEM(field_state.shape, BF16),
            pltpu.VMEM(reservoir_state.shape, BF16),
        ),
        in_specs=[hbm] * 8,
        out_specs=(vmem, vmem),
        scratch_shapes=[
            pltpu.SMEM((2, 2, 8), jnp.int32),
            pltpu.SMEM((2, 8), jnp.int32),
            pltpu.SMEM((2,), jnp.int32),
            pltpu.VMEM(field_state.shape, BF16),
            pltpu.VMEM(reservoir_state.shape, BF16),
            pltpu.VMEM(coupling_blocks.shape, BF16),
            pltpu.VMEM(input_blocks.shape, BF16),
            pltpu.VMEM(readout.shape, BF16),
            pltpu.VMEM(input_blocks.shape, BF16),
            pltpu.VMEM((2, 1024, 384), BF16),
            pltpu.VMEM((8, 2 * ROWS, 128), BF16),
            pltpu.VMEM((2, 8, ROWS, 128), F32),
            pltpu.VMEM((30, ROWS, 128), BF16),
            pltpu.VMEM((STEPS, 4, 3, ROWS, 128), BF16),
            pltpu.VMEM((STEPS, 2, 3, ROWS, 128), BF16),
            pltpu.VMEM((2, 4, 3, 16, 128), BF16),
            pltpu.VMEM((4, 4, 3, 16, 128), BF16),
            pltpu.VMEM((2, 2, 2, 4, 1024), BF16),
            pltpu.VMEM((9 * ROWS, 128), F32),
            pltpu.VMEM((9 * ROWS, 128), F32),
            pltpu.VMEM((2, 144, 128), F32),
            pltpu.VMEM((2, 144, 128), F32),
            pltpu.SemaphoreType.DMA((9,)),
            pltpu.SemaphoreType.DMA((STEPS, 10)),
            pltpu.SemaphoreType.DMA((STEPS, 10)),
            pltpu.SemaphoreType.REGULAR,
        ],
        compiler_params=pltpu.CompilerParams(
            collective_id=0, has_side_effects=True, vmem_limit_bytes=32 * 1024 * 1024
        ),
        name="forecast",
    )(
        *(
            pltpu.with_memory_space_constraint(x, pltpu.HBM)
            for x in (
                jnp.swapaxes(coupling_index, 1, 2), input_index, region_band,
                field_state, reservoir_state, coupling_blocks, input_blocks, readout,
            )
        )
    )
    return pl.pallas_call(
        deliver,
        out_shape=(
            jax.ShapeDtypeStruct(field_state.shape, BF16),
            jax.ShapeDtypeStruct(reservoir_state.shape, BF16),
        ),
        in_specs=[vmem] * 2,
        out_specs=(hbm, hbm),
        scratch_shapes=[pltpu.SemaphoreType.DMA((2,))],
        compiler_params=pltpu.CompilerParams(vmem_limit_bytes=32 * 1024 * 1024),
        name="deliver",
    )(*(pltpu.with_memory_space_constraint(x, pltpu.VMEM) for x in (field, state)))


def solution(mesh):
    return jax.shard_map(
        per_device,
        mesh=mesh,
        in_specs=(
            P(None, "lat", "lon"),
            P("lat", "lon", None, None),
            P("lat", None, None),
            P("lat", None, None),
            P("lat", None, None),
            P("lat", None),
            P("lat", None, None),
            P("lat"),
        ),
        out_specs=(P(None, "lat", "lon"), P("lat", "lon", None, None)),
        check_vma=False,
    )
```

```python
import functools

import jax
import jax.numpy as jnp
from jax import lax
from jax.experimental import pallas as pl
from jax.experimental.pallas import tpu as pltpu
from jax.sharding import PartitionSpec as P

MESH = pl.DeviceIdType.MESH
STEPS = 3
F32 = jnp.float32
BF16 = jnp.bfloat16
TILES = 10
ROWS = 8 * TILES

DIRS = ((-1, 0), (1, 0), (0, -1), (0, 1), (-1, -1), (-1, 1), (1, -1), (1, 1))


def dot_nt(x, w):
    return lax.dot_general(x, w, (((1,), (1,)), ((), ())), preferred_element_type=F32)


def row_of(column, member):
    at = column + 2
    return at % TILES * 8 + at // TILES * 4 + member


def dot_nn(x, w):
    return lax.dot_general(x, w, (((1,), (0,)), ((), ())), preferred_element_type=F32)


def lanes(rows):
    return lax.broadcasted_iota(jnp.int32, (rows, 128), 1)


def roll(x, by):
    return pltpu.roll(x, by, 1)


def minus_parts(r0, r1, r2):
    lane = lanes(r0.shape[0])
    b0 = jnp.where(lane < 48, roll(r0, 48), roll(r1, 48))
    r2r = roll(r2, 80)
    b2 = jnp.where(lane < 80, roll(r1, 80), r2r)
    return b0, b2, r2r


def plus_parts(r0, r1):
    r0r = roll(r0, 112)
    return r0r, r0r, roll(r1, 16)


def windows(r0, r1, r2, n):
    rows = 8 * n
    lane = lanes(rows)
    m = slice(0, rows)
    c = slice(8, rows + 8)
    p = slice(16, rows + 16)
    m0, m2, m3 = minus_parts(r0[m], r1[m], r2[m])
    p1, p2, p4 = plus_parts(r0[p], r1[p])
    c0 = roll(r0[c], 80)
    c1 = roll(r1[c], 80)
    d1 = roll(r1[c], 112)
    d2 = roll(r2[c], 112)
    b0 = jnp.where(lane < 80, m0, c0)
    b1 = jnp.where(lane < 80, c0, jnp.where(lane < 112, c1, p1))
    b2 = jnp.where(lane < 64, p2, m2)
    b3 = jnp.where(lane < 16, m3, jnp.where(lane < 112, d1, d2))
    b4 = jnp.where(lane < 48, d2, p4)
    return b0, b1, b2, b3, b4


def kernel(
    cidx_hbm, qidx_hbm, rband_hbm,
    field_hbm, state_hbm, coup_hbm, drive_hbm, read_hbm,
    field_out, state_out,
    cidx, qidx, rband,
    field_in, state_in, coup, drive, read, coup_t, drive_t, read_t,
    states, pre, win, raw, halo, edge, edge_in, state_edge, ta, tb, ea, eb,
    local_sem, send_sem, recv_sem, ready,
):
    lat, lon = lax.axis_index("lat"), lax.axis_index("lon")
    nlat, nlon = lax.axis_size("lat"), lax.axis_size("lon")
    west, east = lax.rem(lon + nlon - 1, nlon), lax.rem(lon + 1, nlon)
    has_south = lat > 0
    has_north = lat < nlat - 1

    def target(d):
        dl, do = DIRS[d]
        return (lat + dl, west if do < 0 else (east if do > 0 else lon))

    def by_side(fn, dirs=range(8)):
        for d in dirs:
            dl = DIRS[d][0]
            if dl == 0:
                fn(d)
            else:
                pl.when(has_south if dl < 0 else has_north)(functools.partial(fn, d))

    loads = [
        pltpu.make_async_copy(src, dst, local_sem.at[n])
        for n, (src, dst) in enumerate(
            ((field_hbm.at[:, :, 2048:2560], field_in.at[:, :, 2048:2560]),
             (field_hbm.at[:, :, 0:2048], field_in.at[:, :, 0:2048]),
             (state_hbm, state_in), (coup_hbm, coup), (drive_hbm, drive), (read_hbm, read),
             (cidx_hbm, cidx), (qidx_hbm, qidx), (rband_hbm, rband))
        )
    ]
    loads[0].start()

    is_first = lon == 0
    is_last = lon == nlon - 1
    is_before_last = lon == nlon - 2
    greeted = 1 + has_south.astype(jnp.int32) + has_north.astype(jnp.int32)

    barrier = pltpu.get_barrier_semaphore()

    def greet(d):
        pl.semaphore_signal(barrier, inc=1, device_id=target(d), device_id_type=MESH)

    by_side(greet, (4, 6, 2))

    @pl.when(jnp.logical_not(is_last))
    def _():
        by_side(greet, (0, 1))
        pl.when(jnp.logical_not(is_before_last))(lambda: by_side(greet, (5, 7, 3)))

    for load in loads[1:]:
        load.start()

    def remote(src, dst, step, n, d):
        return pltpu.make_async_remote_copy(
            src_ref=src, dst_ref=dst, send_sem=send_sem.at[step, n], recv_sem=recv_sem.at[step, n],
            device_id=target(d), device_id_type=MESH,
        )

    def message(step, d):
        if d == 0:
            return remote(raw.at[step, 0], halo.at[step, 1], step, d, d)
        if d == 1:
            return remote(raw.at[step, 3], halo.at[step, 0], step, d, d)
        dl, do = DIRS[d]
        side, into = (0, 1) if do < 0 else (1, 0)
        if dl == 0:
            return remote(edge.at[side], edge_in.at[into], step, d, d)
        pair = 0 if dl < 0 else 3
        return remote(edge.at[side, pair], edge_in.at[2 + into, pair], step, d, d)

    def lat_part(step, d, n):
        pair, side = (0, 1) if d == 0 else (3, 0)
        blocks = pl.ds(2 * n, 2 - n)
        return remote(raw.at[step, pair, blocks], halo.at[step, side, blocks], step, d + 4 * n, d)

    def state_message(d):
        side, into = (0, 1) if DIRS[d][1] < 0 else (1, 0)
        return remote(state_hbm.at[:, pl.ds(14 * side, 2)], state_edge.at[into], 0, 6 + d, d)

    def wait_recv(step, dirs):
        for d in dirs:
            dl = DIRS[d][0]
            if dl == 0:
                message(step, d).wait_recv()
            else:
                pl.when(has_north if dl < 0 else has_south)(message(step, d).wait_recv)

    def put_raw(step, pair, r):
        for k in range(3):
            raw[step, pair, k] = r[k].astype(BF16)

    @pl.when(is_last)
    def _():
        pl.semaphore_wait(barrier, greeted)
        state_message(3).start()

    lane8 = lanes(8)

    def to_regions(columns, row, stride, to_a, to_b):
        for m in range(4):
            f = {}
            for j in columns:
                q, off = (160 * j) // 128, (160 * j) % 128
                for k in (q, q + 1):
                    if k not in f:
                        f[k] = field_in[m, :, 128 * k:128 * (k + 1)].astype(F32)
                if off == 0:
                    w0, w1 = f[q], f[q + 1]
                else:
                    w1 = roll(f[q + 1], 128 - off)
                    w0 = jnp.where(lane8 < 128 - off, roll(f[q], 128 - off), w1)
                to_a[pl.ds(row(j, m), 8, stride=stride), :] = w0
                to_b[pl.ds(row(j, m), 8, stride=stride), :] = w1

    def to_pair(p, rows, from_a, from_b):
        lane = lanes(rows)
        lo, mid, hi = 2 * p * rows, (2 * p + 1) * rows, (2 * p + 2) * rows
        a0, a1 = from_a[lo:mid], from_b[lo:mid]
        b0, b1 = roll(from_a[mid:hi], 32), roll(from_b[mid:hi], 32)
        return a0, jnp.where(lane < 32, a1, b0), jnp.where(lane < 32, b0, b1)

    def put_edge(side, first):
        to_regions(range(first, first + 3), lambda j, m: 4 * (j - first) + m, 16, ea.at[side], eb.at[side])
        for p in range(4):
            for k, rows in enumerate(to_pair(p, 16, ea.at[side], eb.at[side])):
                edge[side, p, k] = rows.astype(BF16)

    def start(d):
        message(0, d).start()

    loads[0].wait()
    put_edge(1, 13)
    pl.when(is_last)(lambda: by_side(start, (5, 7, 3)))
    loads[1].wait()
    put_edge(0, 0)
    to_regions(range(16), row_of, ROWS, ta, tb)
    for p in range(4):
        put_raw(0, p, to_pair(p, ROWS, ta, tb))

    @pl.when(lat == 0)
    def _():
        halo[:, 0] = jnp.zeros(halo.shape[:1] + halo.shape[2:], BF16)
        edge_in[2:4, 3] = jnp.zeros((2,) + edge_in.shape[2:], BF16)

    @pl.when(lat == nlat - 1)
    def _():
        halo[:, 1] = jnp.zeros(halo.shape[:1] + halo.shape[2:], BF16)
        edge_in[2:4, 0] = jnp.zeros((2,) + edge_in.shape[2:], BF16)

    def send_west():
        by_side(start, (4, 6, 2))
        state_message(2).start()

    @pl.when(is_last)
    def _():
        pl.semaphore_wait(ready, 1)
        by_side(start, (0, 1))
        send_west()

    @pl.when(jnp.logical_not(is_last))
    def _():
        pl.semaphore_wait(barrier, 2 * greeted - 1 + jnp.where(is_first, 0, greeted))

        @pl.when(is_before_last)
        def _():
            pl.semaphore_signal(ready, inc=1, device_id=(lat, east), device_id_type=MESH)

        by_side(start, (5, 7, 3))
        state_message(3).start()
        by_side(start, (0, 1))
        pl.when(jnp.logical_not(is_first))(send_west)

    def put_state(i, t):
        tiles = []
        for s in (t, t + 1):
            tiles.append(state_in[i, s - 2] if s >= 2 else state_edge[0, i, s])
            tiles.append(state_in[i, s + 8] if s < 8 else state_edge[1, i, s - 8])
        rows = jnp.concatenate([x.astype(F32) for x in tiles], axis=0).astype(BF16)
        for c in range(8):
            states[c, ROWS * i + 8 * t:ROWS * i + 8 * t + 16] = rows[:, 128 * c:128 * (c + 1)]

    loads[2].wait()
    for i in range(2):
        for t in (2, 4, 6):
            put_state(i, t)
    for load in loads[3:]:
        load.wait()
    bands = [rband[i] for i in range(2)]

    for band in range(2):
        for b in range(16):
            coup_t[band, 128 * b:128 * (b + 1)] = coup[band, 128 * b:128 * (b + 1)].T
        for b in range(8):
            drive_t[band, 128 * b:128 * (b + 1)] = drive[band, 128 * b:128 * (b + 1)].T
    for h in range(2):
        for c in range(8):
            part = read[0, 320 * h:320 * h + 320, 128 * c:128 * (c + 1)]
            part = jnp.concatenate([part, jnp.zeros((64, 128), BF16)], axis=0)
            read_t[h, 128 * c:128 * (c + 1)] = part.T

    def put_windows(at, ext):
        for k, block in enumerate(windows(*ext, TILES)):
            win[at + k] = block.astype(BF16)

    def western(r, w):
        return jnp.concatenate(
            [w[0:4], r[72:76], w[4:8], r[4:8], w[8:12], r[12:16], r[16:40]], axis=0
        )

    def eastern(r, x):
        return jnp.concatenate(
            [r[24:64], r[64:68], x[0:4], r[72:76], x[4:8], r[4:8], x[8:12]], axis=0
        )

    starts = [(5 + 5 * p, raw.at[0, p], 0, p) for p in range(4)]
    starts += [(0, halo.at[0, 0], 2, 3), (25, halo.at[0, 1], 2, 0)]

    def put_start_windows(pairs, side, tiles, at, rows):
        for to, ref, edges, p in pairs:
            ext = [tiles(ref[k].astype(F32), edge_in[edges + side, p, k].astype(F32)) for k in range(3)]
            for k, block in enumerate(windows(*ext, rows // 8)):
                win[to + k, at:at + rows] = block.astype(BF16)

    def without_edges(r):
        return jnp.concatenate([r[72:76], r[72:76], r, r[4:8], r[4:8]], axis=0)

    near = jnp.where(lat < nlat // 2, 0, 1)
    for step in range(STEPS):
        if step == 0:
            state_message(2).wait_recv()
            for i in range(2):
                put_state(i, 8)
            wait_recv(step, (2,))
            put_start_windows(starts[:4], 1, eastern, 32, 48)
            wait_recv(step, (0, 1, 4, 6))
            put_start_windows(starts[4:], 1, eastern, 32, 48)
            state_message(3).wait_recv()
            for i in range(2):
                put_state(i, 0)
        for i in range(2):
            for b in range(8):
                x = jnp.concatenate(
                    [states[cidx[bands[i], k, b], ROWS * i:ROWS * (i + 1)] for k in range(2)], axis=1
                )
                pre[i, b] = dot_nn(x, coup_t[bands[i], 256 * b:256 * (b + 1)])
        if step == 0:
            wait_recv(step, (3, 5, 7))
            put_start_windows(starts, 0, western, 0, 32)
        else:
            for p in range(4):
                put_windows(5 + 5 * p, [without_edges(raw[step, p, k].astype(F32)) for k in range(3)])

        def put_halo_windows(i):
            put_windows(25 * i, [without_edges(halo[step, i, k].astype(F32)) for k in range(3)])

        def put_new_states(i):
            band = rband[i]
            rows = pl.ds(pl.multiple_of(ROWS * i, ROWS), ROWS)
            for b in range(8):
                x = win[10 * i + qidx[band, b]]
                w = drive_t[band, 128 * b:128 * (b + 1)]
                new = jnp.tanh(pre[i, b] + dot_nn(x, w))
                states[b, rows] = new.astype(BF16)
                if step == STEPS - 1:
                    for j in range(16):
                        at = row_of(j, 0)
                        state_out[i, j, :, 128 * b:128 * (b + 1)] = new[at:at + 4].astype(BF16)

        if step == 0:
            for i in range(2):
                put_new_states(i)
        else:
            for turn in range(2):
                i = near if turn == 0 else 1 - near
                for n in range(2):
                    pl.when((i == 0) & has_south)(lat_part(step, 1, n).wait_recv)
                    pl.when((i == 1) & has_north)(lat_part(step, 0, n).wait_recv)
                put_halo_windows(i)
                put_new_states(i)
        x = jnp.concatenate([states[c] for c in range(8)], axis=1)
        if step < STEPS - 1:
            far = 1 - near

            def put(i, h, y, first=0):
                for k in range(y.shape[1] // 128):
                    raw[step + 1, 2 * i + h, first + k] = y[:, 128 * k:128 * (k + 1)].astype(BF16)

            def go(h, parts):
                for n in parts:
                    pl.when((h == 0) & has_south)(lat_part(step + 1, 0, n).start)
                    pl.when((h == 1) & has_north)(lat_part(step + 1, 1, n).start)

            far_rows = pl.ds(pl.multiple_of(ROWS * far, ROWS), ROWS)
            x_far = jnp.concatenate([states[c, far_rows] for c in range(8)], axis=1)
            put(far, far, dot_nn(x_far, read_t[far, :, 0:256]))
            go(far, (0,))
            put(far, far, dot_nn(x_far, read_t[far, :, 256:384]), 2)
            go(far, (1,))
            y = dot_nn(x, read_t[near])
            for i in range(2):
                put(i, near, y[ROWS * i:ROWS * (i + 1)])
            go(near, (0, 1))
            near_rows = pl.ds(pl.multiple_of(ROWS * near, ROWS), ROWS)
            x_near = jnp.concatenate([states[c, near_rows] for c in range(8)], axis=1)
            put(near, far, dot_nn(x_near, read_t[far]))
            if step == 0:
                pl.when(is_first)(send_west)
        else:
            lane = lanes(ROWS)
            for h in range(2):
                y = dot_nn(x, read_t[h])
                for i in range(2):
                    y0, y1, y2 = (y[ROWS * i:ROWS * (i + 1), 128 * k:128 * (k + 1)] for k in range(3))
                    at = ROWS * (4 * i + 2 * h)
                    ta[at:at + ROWS] = y0
                    tb[at:at + ROWS] = y1
                    r1, r2 = roll(y1, 96), roll(y2, 96)
                    ta[at + ROWS:at + 2 * ROWS] = jnp.where(lane < 96, r1, r2)
                    tb[at + ROWS:at + 2 * ROWS] = r2

    for m in range(4):
        cols = []
        prev = None
        for j in range(16):
            off = (160 * j) % 128
            v0 = ta[pl.ds(row_of(j, m), 8, stride=ROWS), :]
            v1 = tb[pl.ds(row_of(j, m), 8, stride=ROWS), :]
            if off == 0:
                cols.append(v0)
                prev = (v0, v1, 0)
                continue
            r0, r1 = roll(v0, off), roll(v1, off)
            p0, p1, po = prev
            cols.append(jnp.where(lane8 < po, p0, jnp.where(lane8 < po + 32, p1, r0)))
            prev = (r0, r1, off)
            if off == 96:
                cols.append(jnp.where(lane8 < 96, r0, r1))
        for k in range(20):
            field_out[m, :, 128 * k:128 * (k + 1)] = cols[k].astype(BF16)

    by_side(lambda d: message(0, d).wait_send())
    for d in (2, 3):
        state_message(d).wait_send()
    for step in range(1, STEPS):
        for n in range(2):
            by_side(lambda d: lat_part(step, d, n).wait_send(), (0, 1))


def deliver(field_ref, state_ref, field_out, state_out, sems):
    copies = [
        pltpu.make_async_copy(field_ref, field_out, sems.at[0]),
        pltpu.make_async_copy(state_ref, state_out, sems.at[1]),
    ]
    for copy in copies:
        copy.start()
    for copy in copies:
        copy.wait()


def per_device(field_state, reservoir_state, coupling_blocks, coupling_index, input_blocks, input_index, readout, region_band):
    hbm = pl.BlockSpec(memory_space=pltpu.HBM)
    vmem = pl.BlockSpec(memory_space=pltpu.VMEM)
    field, state = pl.pallas_call(
        kernel,
        out_shape=(
            pltpu.VMEM(field_state.shape, BF16),
            pltpu.VMEM(reservoir_state.shape, BF16),
        ),
        in_specs=[hbm] * 8,
        out_specs=(vmem, vmem),
        scratch_shapes=[
            pltpu.SMEM((2, 2, 8), jnp.int32),
            pltpu.SMEM((2, 8), jnp.int32),
            pltpu.SMEM((2,), jnp.int32),
            pltpu.VMEM(field_state.shape, BF16),
            pltpu.VMEM(reservoir_state.shape, BF16),
            pltpu.VMEM(coupling_blocks.shape, BF16),
            pltpu.VMEM(input_blocks.shape, BF16),
            pltpu.VMEM(readout.shape, BF16),
            pltpu.VMEM(coupling_blocks.shape, BF16),
            pltpu.VMEM(input_blocks.shape, BF16),
            pltpu.VMEM((2, 1024, 384), BF16),
            pltpu.VMEM((8, 2 * ROWS, 128), BF16),
            pltpu.VMEM((2, 8, ROWS, 128), F32),
            pltpu.VMEM((30, ROWS, 128), BF16),
            pltpu.VMEM((STEPS, 4, 3, ROWS, 128), BF16),
            pltpu.VMEM((STEPS, 2, 3, ROWS, 128), BF16),
            pltpu.VMEM((2, 4, 3, 16, 128), BF16),
            pltpu.VMEM((4, 4, 3, 16, 128), BF16),
            pltpu.VMEM((2, 2, 2, 4, 1024), BF16),
            pltpu.VMEM((9 * ROWS, 128), F32),
            pltpu.VMEM((9 * ROWS, 128), F32),
            pltpu.VMEM((2, 144, 128), F32),
            pltpu.VMEM((2, 144, 128), F32),
            pltpu.SemaphoreType.DMA((9,)),
            pltpu.SemaphoreType.DMA((STEPS, 10)),
            pltpu.SemaphoreType.DMA((STEPS, 10)),
            pltpu.SemaphoreType.REGULAR,
        ],
        compiler_params=pltpu.CompilerParams(
            collective_id=0, has_side_effects=True, vmem_limit_bytes=32 * 1024 * 1024
        ),
        name="forecast",
    )(
        *(
            pltpu.with_memory_space_constraint(x, pltpu.HBM)
            for x in (
                jnp.swapaxes(coupling_index, 1, 2), input_index, region_band,
                field_state, reservoir_state, coupling_blocks, input_blocks, readout,
            )
        )
    )
    return pl.pallas_call(
        deliver,
        out_shape=(
            jax.ShapeDtypeStruct(field_state.shape, BF16),
            jax.ShapeDtypeStruct(reservoir_state.shape, BF16),
        ),
        in_specs=[vmem] * 2,
        out_specs=(hbm, hbm),
        scratch_shapes=[pltpu.SemaphoreType.DMA((2,))],
        compiler_params=pltpu.CompilerParams(vmem_limit_bytes=32 * 1024 * 1024),
        name="deliver",
    )(*(pltpu.with_memory_space_constraint(x, pltpu.VMEM) for x in (field, state)))


def solution(mesh):
    return jax.shard_map(
        per_device,
        mesh=mesh,
        in_specs=(
            P(None, "lat", "lon"),
            P("lat", "lon", None, None),
            P("lat", None, None),
            P("lat", None, None),
            P("lat", None, None),
            P("lat", None),
            P("lat", None, None),
            P("lat"),
        ),
        out_specs=(P(None, "lat", "lon"), P("lat", "lon", None, None)),
        check_vma=False,
    )
```
